32 devices in a mesh: post: 16 (over z, x, core), rep: 2 (over y).
Axes of the slice: x: 2, y: 2, z: 4, core: 2. Of those that a mesh axis runs over, the one named last changes fastest.
Arguments:
- split_vectors: bfloat16 [512, 192, 1024], P('post', None, 'rep'), may hold values from -6 to 6
- split_labels: int32 [512, 192], P('post'), may hold values from 0 to 1, as said below
- split_lengths: int32 [512], P('post'), may hold values from 144 to 192
- new_owners: int32 [512, 2], P('post'), may hold values from 0 to 15, all different within a row; in each aligned block of 32 rows (0 to 31, 32 to 63, ...) at most 8 rows name the same one
- neighbour_ids: int32 [512, 64], replicated, may hold values from 0 to 127, all different within a row
- resident_vectors: bfloat16 [128, 192, 1024], P('post', None, 'rep'), may hold values from -6 to 6
- resident_centroids: bfloat16 [128, 1024], P('post', 'rep'), may hold values from -1 to 1
- resident_lengths: int32 [128], P('post'), may hold values from 1 to 192
Outputs:
- new_postings: bfloat16 [256, 8, 96, 1024], P('post', None, None, 'rep')
- new_centroids: float32 [512, 2, 1024], P('post', None, 'rep')
- rescore: float32 [128, 192], P('post')
The draws below stay inside these ranges and needn't reach their ends.
Inputs may be any that keep to these rules, and one draw needn't show every extreme that they name: `split_labels`: rows at or past a posting's length carry label 1; each half of a split posting holds between 48 and 96 valid rows, and some split has both halves of exactly 96 rows. `new_owners`: the two halves of a split go to different owners; the halves of the splits of one index of post give at most 8 to any one owner. `neighbour_ids`: each split names 64 different postings.
All inputs are finite; a program needn't handle non-finite values.
Results may differ from the reference program's by a relative error of at most 0.0034.
Values may be sent and summed in bfloat16 or wider, within the bound.
A program may use at most 128 MiB of HBM per device.

```python
import math
import jax
import jax.numpy as jnp
import numpy as np
from jax import lax

D = 1024
L = 192
NEIGH = 64
S_DEV = 32
HALF = 96
HSLOT = 8
SPLITS = 512
RES = 128
N_POST = 16


def split_shared(key):
    base_key = jax.random.fold_in(key, 7)
    key_length, key_first, key_order = jax.random.split(base_key, 3)
    split_ids = jnp.arange(SPLITS)
    lengths = jax.random.randint(key_length, (SPLITS,), 3 * HALF // 2, L + 1)
    lengths = jnp.where(split_ids % 8 == 0, L, lengths)
    lowest = lengths - HALF
    first_count = lowest + jax.random.randint(key_first, (SPLITS,), 0, 1 << 20) % (HALF - lowest + 1)
    first_count = jnp.where(split_ids % 8 == 0, HALF, first_count)

    def shuffled(row_key):
        return jax.random.permutation(row_key, L)
    scores = jax.vmap(shuffled)(jax.random.split(key_order, SPLITS))
    row_ids = jnp.arange(L)
    scores = jnp.where(row_ids[None, :] < lengths[:, None], scores, L + row_ids[None, :])
    ranking = jnp.argsort(jnp.argsort(scores, axis=1, stable=True), axis=1, stable=True)
    labels = (ranking >= first_count[:, None]).astype(jnp.int32)
    return (lengths.astype(jnp.int32), labels)


def draw_split_lengths(key, part):
    return split_shared(key)[0]


def draw_split_labels(key, part):
    return split_shared(key)[1]


def place_ends(drawn, stream_key, least, high):
    shape = drawn.shape
    spot = [jax.random.randint(jax.random.fold_in(stream_key, axis), (), 0, shape[axis]) for axis in range(len(shape))]
    drawn = drawn.at[tuple(spot)].set(least)
    longest = shape.index(max(shape))
    spot[longest] = (spot[longest] + 1) % shape[longest]
    return drawn.at[tuple(spot)].set(high)


def steps_of(own_key, shape, cuts, smallest, top_value):
    gain = 1.0
    for axis_at, shards_of in cuts:
        draws = jax.random.uniform(jax.random.fold_in(jax.random.fold_in(own_key, 6), axis_at), (shards_of,), jnp.float32, smallest / len(cuts), top_value / len(cuts))
        gain = gain * jnp.repeat(jnp.exp(draws), shape[axis_at] // shards_of).reshape((-1,) + (1,) * (len(shape) - 1 - axis_at))
    return gain


def different_ones(rng, rows, amount, top, lift):
    order = jax.random.permutation(jax.random.fold_in(rng, 1), amount)
    favour = order
    for power in range(3):
        favour = favour * favour // amount
    favour = favour * lift // amount
    tickets = jax.random.randint(jax.random.fold_in(rng, 2), (rows, amount), 0, 4096) + favour
    fixed_rows = jax.random.permutation(jax.random.fold_in(rng, 3), rows)[jnp.arange(amount) % rows]
    tickets = jnp.where(jnp.arange(rows)[:, None] == fixed_rows[None, :], 1 << 14, tickets)
    merit = tickets * amount + jnp.arange(amount)
    return lax.top_k(merit.astype(jnp.int32), top)[1].astype(jnp.int32)


def assign_block(key, own, number, rows, amount, top, reach, lean):
    sequence = jax.random.permutation(key, amount)
    crowded, common = shares(amount, rows * top, reach, lean, True), shares(amount, rows * top, reach, lean, False)
    places = jnp.arange(amount)

    def named(sizes, turn):
        used = int((sizes > 0).sum())
        fixed = max(1, used // 4)
        shifted = fixed + (places - fixed + turn * (used - fixed)) % max(1, amount - fixed)
        return jnp.zeros((amount,), jnp.int32).at[sequence[jnp.where(places < fixed, places, shifted)]].set(jnp.asarray(sizes, jnp.int32))

    sizes = jnp.where(number % 4 == 0, named(crowded, number // 4), named(common, number - number // 4 - 1))
    mixed = jax.random.permutation(jax.random.fold_in(own, 3), amount)
    source_of, taker = mixed[0:amount // 2 * 2:2], mixed[1:amount // 2 * 2:2]
    margin = jnp.minimum(sizes[source_of] - 1, reach - sizes[taker]) // 2
    margin = jnp.where((source_of == sequence[0]) | (taker == sequence[0]) | (sizes[taker] == 0), 0, jnp.maximum(margin, 0))
    shifted = jax.random.randint(jax.random.fold_in(own, 4), (amount // 2,), 0, 1 << 20) % (margin + 1)
    sizes = sizes.at[source_of].add(-shifted).at[taker].add(shifted)
    items = jnp.searchsorted(jnp.cumsum(sizes), jnp.arange(rows * top), side="right").astype(jnp.int32)
    listing = items.reshape(top, rows).T
    listing = listing[jax.random.permutation(jax.random.fold_in(own, 1), rows)]
    turn = jax.random.randint(jax.random.fold_in(own, 2), (rows, 1), 0, top)
    return jnp.take_along_axis(listing, (jnp.arange(top)[None, :] + turn) % top, axis=1)


def shares(count, total, most, lean, full):
    portions = [(1 << 20) // math.isqrt(rank ** lean) + 1 for rank in range(1, count + 1)]
    largest = most if full else min(most, max(-(-total // count), total * portions[0] // sum(portions)))
    least = 1 if total - largest >= count - 1 else 0
    holding, rest = [largest] + [least] * (count - 1), total - largest - least * (count - 1)
    while rest > 0:
        free = [i for i in range(1, count) if holding[i] < largest] or [i for i in range(1, count) if holding[i] < most]
        mass, left = sum([portions[i] for i in free]), rest
        for i in free:
            addition = min(most - holding[i], max(1, left * portions[i] // mass), rest)
            holding[i] = holding[i] + addition
            rest = rest - addition
    return np.array(holding)


def gaussian(key, dims, spread, limit, cuts=(), kind=jnp.bfloat16):
    values = jax.random.normal(key, dims, jnp.float32) * spread
    if len(cuts) > 0:
        values = steps_of(key, dims, cuts, -0.22, 0.18) * values
    return jnp.clip(values, min=-limit, max=limit).astype(kind)


def setup_inputs(seed: int = 0) -> dict:
    streams_of = jax.random.split(jax.random.key(seed), 9)
    split_vectors = gaussian(streams_of[0], (SPLITS, L, D), 1.0, 6.0, ((0, 16), (2, 2)))
    split_labels = draw_split_labels(jax.random.fold_in(streams_of[8], 71), 0)
    split_lengths = draw_split_lengths(jax.random.fold_in(streams_of[8], 71), 0)
    new_owners_keys = jax.random.split(jax.random.fold_in(streams_of[3], 1), SPLITS // S_DEV)
    new_owners_turns = jax.random.permutation(jax.random.fold_in(streams_of[3], 3), SPLITS // S_DEV)
    new_owners = jax.vmap(lambda own, number: assign_block(jax.random.fold_in(streams_of[3], 2), own, number, S_DEV, N_POST, 2, HSLOT, 2))(new_owners_keys, new_owners_turns).reshape((SPLITS, 2))
    neighbour_ids = different_ones(streams_of[4], SPLITS, RES, NEIGH, 0)
    resident_vectors = gaussian(streams_of[5], (RES, L, D), 1.0, 6.0, ((0, 16), (2, 2)))
    resident_centroids = gaussian(streams_of[6], (RES, D), 0.15, 1.0, ((0, 16), (1, 2)))
    resident_lengths = place_ends(jax.random.randint(streams_of[7], (RES,), 1, L + 1), jax.random.fold_in(streams_of[7], 1), 1, L).astype(jnp.int32)
    return {"split_vectors": split_vectors, "split_labels": split_labels, "split_lengths": split_lengths, "new_owners": new_owners, "neighbour_ids": neighbour_ids, "resident_vectors": resident_vectors, "resident_centroids": resident_centroids, "resident_lengths": resident_lengths}


far_value = 1e+30

def pack_split(inputs):
    vectors, labels, length = inputs
    row_ids = jnp.arange(L)
    in_half = (row_ids[None, :] < length) & (labels[None, :] == jnp.arange(2)[:, None])
    member_int = in_half.astype(jnp.int32)
    half_rank = jnp.cumsum(member_int, axis=1) - member_int
    placement = in_half[:, None, :] & (half_rank[:, None, :] == jnp.arange(HALF)[None, :, None])
    packed = jnp.dot(placement.reshape(2 * HALF, L).astype(jnp.bfloat16), vectors, preferred_element_type=jnp.float32)
    packed = packed.astype(jnp.bfloat16).reshape(2, HALF, D)
    half_sums = jnp.dot(in_half.astype(jnp.bfloat16), vectors, preferred_element_type=jnp.float32)
    counts = lax.optimization_barrier(jnp.sum(member_int, axis=1)).astype(jnp.float32)
    return (packed, half_sums / counts[:, None])

def reference(split_vectors, split_labels, split_lengths, new_owners, neighbour_ids, resident_vectors, resident_centroids, resident_lengths):
    packed, new_centroids = lax.map(pack_split, (split_vectors, split_labels, split_lengths))
    owner_blocks = new_owners.reshape(N_POST, 2 * S_DEV).astype(jnp.int32)
    half_order = jnp.arange(2 * S_DEV)
    same_owner = (owner_blocks[:, :, None] == owner_blocks[:, None, :]) & (half_order[None, None, :] < half_order[None, :, None])
    slot_within = lax.optimization_barrier(jnp.sum(same_owner.astype(jnp.int32), axis=2)).astype(jnp.int32)
    source_ids = jnp.arange(N_POST, dtype=jnp.int32)[:, None]
    target_slot = ((owner_blocks * N_POST + source_ids) * HSLOT + slot_within).reshape(-1).astype(jnp.int32)
    stored = jnp.zeros((N_POST * N_POST * HSLOT, HALF, D), jnp.bfloat16)
    stored = stored.at[target_slot].set(packed.reshape(SPLITS * 2, HALF, D))
    new_postings = stored.reshape(N_POST * N_POST, HSLOT, HALF, D)
    centroid_b = new_centroids.astype(jnp.bfloat16).reshape(2 * SPLITS, D)
    centroid_wide = centroid_b.astype(jnp.float32)
    centroid_norm = lax.optimization_barrier(jnp.sum(centroid_wide * centroid_wide, axis=1))
    split_ids = jnp.broadcast_to(jnp.arange(SPLITS, dtype=jnp.int32)[:, None], (SPLITS, NEIGH))
    named = jnp.zeros((SPLITS, RES), jnp.int32).at[split_ids, neighbour_ids.astype(jnp.int32)].set(1)
    named = jnp.repeat(named, 2, axis=0).T

    def score_one(inputs):
        vectors, current, length, hit = inputs
        vector_wide = vectors.astype(jnp.float32)
        own_diff = vector_wide - current.astype(jnp.float32)[None, :]
        own = lax.optimization_barrier(jnp.sum(own_diff * own_diff, axis=1))
        row_norm = lax.optimization_barrier(jnp.sum(vector_wide * vector_wide, axis=1))
        cross = jnp.dot(vectors, centroid_b.T, preferred_element_type=jnp.float32)
        distance = row_norm[:, None] - 2.0 * cross + centroid_norm[None, :]
        distance = jnp.where(hit[None, :] > 0, distance, far_value)
        best_dist = jnp.minimum(own, lax.optimization_barrier(jnp.min(distance, axis=1)))
        score = (best_dist - row_norm) / math.sqrt(D)
        return jnp.where(jnp.arange(L) < length, score, 0.0)
    rescore = lax.map(score_one, (resident_vectors, resident_centroids, resident_lengths, named))
    return (new_postings, new_centroids, rescore)
```

```python
import functools
import math

import jax
import jax.numpy as jnp
from jax import lax
from jax.experimental import pallas as pl
from jax.experimental.pallas import tpu as pltpu
from jax.sharding import PartitionSpec as P

far_value = 1e30
STEP = 8


def pack_kernel(
    n_halves, n_slots, target_ref, empty_ref, vec_ref, label_ref, length_ref, out_ref, cent_ref, packed, blank, sem
):
    step = pl.program_id(0)
    length = vec_ref.shape[1]
    half_rows = length // 2

    @pl.when(step == 0)
    def _():
        blank[...] = jnp.zeros_like(blank)

        def clear(i, carry):
            pltpu.make_async_copy(blank, out_ref.at[empty_ref[i]], sem).start()
            return carry

        lax.fori_loop(0, n_slots - n_halves, clear, 0)

    labels = label_ref[...]
    valid = lax.broadcasted_iota(jnp.int32, labels.shape, 1) < length_ref[...]
    first = jnp.where(valid & (labels == 0), 1.0, 0.0)
    second = jnp.where(valid & (labels == 1), 1.0, 0.0)
    earlier = lax.broadcasted_iota(jnp.int32, (length, length), 0) < lax.broadcasted_iota(
        jnp.int32, (length, length), 1
    )
    earlier = jnp.where(earlier, 1.0, 0.0).astype(jnp.bfloat16)
    rank_first = jnp.dot(first.astype(jnp.bfloat16), earlier, preferred_element_type=jnp.float32)
    rank_second = jnp.dot(second.astype(jnp.bfloat16), earlier, preferred_element_type=jnp.float32)
    place = jnp.where(first > 0, rank_first, jnp.where(second > 0, half_rows + rank_second, -1.0))
    place = place.astype(jnp.int32)
    count_first = jnp.sum(first, axis=1, keepdims=True)
    count_second = jnp.sum(second, axis=1, keepdims=True)
    row = lax.broadcasted_iota(jnp.int32, (length + 16, length), 0)
    for s in range(STEP):
        chosen = jnp.where(row == place[s : s + 1], 1.0, 0.0)
        chosen = jnp.where(row == length, first[s : s + 1], chosen)
        chosen = jnp.where(row == length + 1, second[s : s + 1], chosen)
        rows = jnp.dot(chosen.astype(jnp.bfloat16), vec_ref[s], preferred_element_type=jnp.float32)
        cent_ref[2 * s : 2 * s + 1] = rows[length : length + 1] / count_first[s : s + 1]
        cent_ref[2 * s + 1 : 2 * s + 2] = rows[length + 1 : length + 2] / count_second[s : s + 1]
        half = (step * STEP + s) * 2
        for h in range(2):
            packed[half + h] = rows[h * half_rows : (h + 1) * half_rows].astype(jnp.bfloat16)
            pltpu.make_async_copy(packed.at[half + h], out_ref.at[target_ref[half + h]], sem).start()

    @pl.when(step == pl.num_programs(0) - 1)
    def _():
        pltpu.make_async_copy(out_ref, out_ref, sem).wait()


def pack(vectors, labels, lengths, target, empty, n_slots):
    s_local, length, dim_share = vectors.shape
    half_rows = length // 2
    return pl.pallas_call(
        functools.partial(pack_kernel, 2 * s_local, n_slots),
        grid_spec=pltpu.PrefetchScalarGridSpec(
            num_scalar_prefetch=2,
            grid=(s_local // STEP,),
            in_specs=[
                pl.BlockSpec((STEP, length, dim_share), lambda i, *_: (i, 0, 0)),
                pl.BlockSpec((STEP, length), lambda i, *_: (i, 0)),
                pl.BlockSpec((STEP, 1), lambda i, *_: (i, 0)),
            ],
            out_specs=[
                pl.BlockSpec(memory_space=pl.ANY),
                pl.BlockSpec((2 * STEP, dim_share), lambda i, *_: (i, 0)),
            ],
            scratch_shapes=[
                pltpu.VMEM((2 * s_local, half_rows, dim_share), jnp.bfloat16),
                pltpu.VMEM((half_rows, dim_share), jnp.bfloat16),
                pltpu.SemaphoreType.DMA,
            ],
        ),
        out_shape=[
            jax.ShapeDtypeStruct((n_slots, half_rows, dim_share), jnp.bfloat16),
            jax.ShapeDtypeStruct((2 * s_local, dim_share), jnp.float32),
        ],
        compiler_params=pltpu.CompilerParams(vmem_limit_bytes=32 * 2**20),
        cost_estimate=pl.CostEstimate(
            flops=2 * s_local * (length + 16) * length * dim_share,
            bytes_accessed=2 * vectors.size + 2 * n_slots * half_rows * dim_share,
            transcendentals=0,
        ),
    )(target, empty, vectors, labels, lengths[:, None])


def routes(new_owners, n_post, hslot):
    owner_flat = new_owners.reshape(-1)
    n_halves = owner_flat.shape[0]
    n_slots = n_post * hslot
    half_order = jnp.arange(n_halves)
    same_owner = (owner_flat[:, None] == owner_flat[None, :]) & (
        half_order[None, :] < half_order[:, None]
    )
    slot_within = jnp.sum(same_owner.astype(jnp.int32), axis=1)
    target = owner_flat * hslot + slot_within
    slot_ids = jnp.arange(n_slots)
    is_empty = ~jnp.any(slot_ids[:, None] == target[None, :], axis=1)
    before = jnp.sum((is_empty[None, :] & (slot_ids[None, :] < slot_ids[:, None])).astype(jnp.int32), axis=1)
    chosen = is_empty[None, :] & (before[None, :] == jnp.arange(n_slots - n_halves)[:, None])
    empty = jnp.sum(jnp.where(chosen, slot_ids[None, :], 0), axis=1)
    return target.astype(jnp.int32), empty.astype(jnp.int32)


def body(
    split_vectors,
    split_labels,
    split_lengths,
    new_owners,
    neighbour_ids,
    resident_vectors,
    resident_centroids,
    resident_lengths,
):
    n_post = lax.axis_size("post")
    s_local, length, dim_share = split_vectors.shape
    half_rows = length // 2
    hslot = max(2, 4 * s_local // n_post)
    res_local = resident_vectors.shape[0]
    n_rep = lax.axis_size("rep")
    res_part = res_local // n_rep
    post_index = lax.axis_index("post")
    rep_index = lax.axis_index("rep")
    mine_at = rep_index * res_part

    def shifted(array, offset):
        if offset == 0:
            return array
        return lax.ppermute(array, "rep", [(i, (i + offset) % n_rep) for i in range(n_rep)])

    def part_of(array, offset):
        at = lax.rem(rep_index + offset, n_rep) * res_part
        return lax.dynamic_slice_in_dim(array, at, res_part, 0)

    rows_shares = [shifted(part_of(resident_vectors, k), k) for k in range(n_rep)]
    current_shares = [shifted(part_of(resident_centroids, k), k) for k in range(n_rep)]

    target, empty = routes(new_owners, n_post, hslot)
    outgoing, centroids = pack(split_vectors, split_labels, split_lengths, target, empty, n_post * hslot)
    new_centroids = centroids.reshape(s_local, 2, dim_share)
    cent_mine = lax.all_gather(centroids.astype(jnp.bfloat16), "post", axis=0, tiled=True)
    outgoing, cent_mine = lax.optimization_barrier((outgoing, cent_mine))
    outgoing = outgoing.reshape(n_post, hslot, half_rows, dim_share)
    new_postings = lax.all_to_all(outgoing, "post", split_axis=0, concat_axis=0, tiled=True)

    cent_shares = [shifted(cent_mine, k) for k in range(n_rep)]
    n_cents = cent_mine.shape[0]
    my_postings = post_index * res_local + mine_at + jnp.arange(res_part)
    hits = jnp.any(neighbour_ids[:, :, None] == my_postings[None, None, :], axis=1)
    hits = jnp.repeat(hits, 2, axis=0).T

    own = 0.0
    row_norm = 0.0
    cent_norm = 0.0
    cross = 0.0
    for rows, current, cents in zip(rows_shares, current_shares, cent_shares):
        wide = rows.astype(jnp.float32)
        gap = wide - current.astype(jnp.float32)[:, None, :]
        own += jnp.sum(gap * gap, axis=2)
        row_norm += jnp.sum(wide * wide, axis=2)
        cents_wide = cents.astype(jnp.float32)
        cent_norm += jnp.sum(cents_wide * cents_wide, axis=1)
        cross += lax.dot_general(
            rows.reshape(res_part * length, dim_share),
            cents,
            (((1,), (1,)), ((), ())),
            preferred_element_type=jnp.float32,
        )
    distance = row_norm[:, :, None] - 2.0 * cross.reshape(res_part, length, n_cents) + cent_norm
    distance = jnp.where(hits[:, None, :], distance, far_value)
    best_dist = jnp.minimum(own, jnp.min(distance, axis=2))
    scores = (best_dist - row_norm) / math.sqrt(n_rep * dim_share)
    lengths_mine = part_of(resident_lengths, 0)
    scores = jnp.where(jnp.arange(length)[None, :] < lengths_mine[:, None], scores, 0.0)
    rescore = lax.all_gather(scores, "rep", axis=0, tiled=True)
    return (new_postings, new_centroids, rescore)


def solution(mesh):
    return jax.shard_map(
        body,
        mesh=mesh,
        in_specs=(
            P("post", None, "rep"),
            P("post", None),
            P("post"),
            P("post", None),
            P(),
            P("post", None, "rep"),
            P("post", "rep"),
            P("post"),
        ),
        out_specs=(P("post", None, None, "rep"), P("post", None, "rep"), P("post", None)),
        check_vma=False,
    )
```

```python
import functools
import math

import jax
import jax.numpy as jnp
from jax import lax
from jax.experimental import pallas as pl
from jax.experimental.pallas import tpu as pltpu
from jax.sharding import PartitionSpec as P

far_value = 1e30
ROWS = 16
GROUP = 4
MESH = pl.DeviceIdType.MESH


def wait_bytes(ref, sem):
    pltpu.make_async_copy(ref, ref, sem).wait()


def exchange_kernel(
    cross_ref,
    near_ref,
    relay_ref,
    vec_ref,
    label_ref,
    length_ref,
    out_ref,
    cent_ref,
    cent_all,
    cent_rep,
    packed,
    place,
    members,
    cross_send,
    near_send,
    relay_send,
    cent_own,
    cent_in,
    cross_sem,
    near_sem,
    relay_sem,
    out_sem,
    cent_sem,
    cent_fwd_sem,
    cent_in_sem,
    cent_all_sem,
    rep_sem,
    rep_in_sem,
    cross_in_sem,
    *cross_in,
):
    n_post = lax.axis_size("post")
    n_rep = lax.axis_size("rep")
    me = lax.axis_index("post")
    rep = lax.axis_index("rep")
    lanes = n_post // 4
    peers = n_post // 2
    side = me // peers
    base = side * peers
    layer = me // lanes
    lane = lax.rem(me, lanes)
    turn = lax.rem(layer, 2)
    relay = (2 - side) * lanes + lane
    is_relay = (layer == 1) | (layer == 2)
    first_source = (1 - side) * peers + lane
    s_local, length, dim_share = vec_ref.shape
    half_rows = length // 2
    n_halves = 2 * s_local
    hslot = out_ref.shape[1]
    capacity = cross_send.shape[1]
    chunks = half_rows // ROWS

    def peer(k):
        return base + lax.rem(me - base + k, peers)

    def post_id(p):
        return {"post": p}

    def rep_id(k):
        return {"rep": lax.rem(rep + k, n_rep)}

    barrier = pltpu.get_barrier_semaphore()

    def greet(k, carry):
        pl.semaphore_signal(barrier, inc=1, device_id=post_id(peer(k)), device_id_type=MESH)
        return carry

    lax.fori_loop(1, peers, greet, 0)
    for k in range(1, n_rep):
        pl.semaphore_signal(barrier, inc=1, device_id=rep_id(k), device_id_type=MESH)

    @pl.when(is_relay)
    def _():
        for j in range(2):
            pl.semaphore_signal(
                barrier, inc=1, device_id=post_id(first_source + j * lanes), device_id_type=MESH
            )

    labels = label_ref[...]
    valid = lax.broadcasted_iota(jnp.int32, labels.shape, 1) < length_ref[...]
    first = jnp.where(valid & (labels == 0), 1.0, 0.0)
    second = jnp.where(valid & (labels == 1), 1.0, 0.0)
    earlier = lax.broadcasted_iota(jnp.int32, (length, length), 0) < lax.broadcasted_iota(
        jnp.int32, (length, length), 1
    )
    earlier = jnp.where(earlier, 1.0, 0.0).astype(jnp.bfloat16)
    rank_first = jnp.dot(first.astype(jnp.bfloat16), earlier, preferred_element_type=jnp.float32)
    rank_second = jnp.dot(second.astype(jnp.bfloat16), earlier, preferred_element_type=jnp.float32)
    spot = jnp.where(first > 0, rank_first, jnp.where(second > 0, half_rows + rank_second, -1.0))
    place[...] = spot.astype(jnp.int32)
    members[0] = first
    members[1] = second

    blank = jnp.zeros((ROWS, dim_share), jnp.bfloat16)
    packed[n_halves] = blank
    for c in range(chunks):
        for j in range(2):
            cross_in[c][j, capacity] = blank

    row = lax.broadcasted_iota(jnp.int32, (2 * ROWS, length), 0)
    row = jnp.where(row < ROWS, row, row - ROWS + half_rows)
    sum_row = lax.broadcasted_iota(jnp.int32, (ROWS, length), 0)

    def pack_chunk(c):
        def group(g, carry):
            for t in range(GROUP):
                s = g * GROUP + t
                chosen = jnp.where(row + c * ROWS == place[pl.ds(s, 1), :], 1.0, 0.0)
                if c == 0:
                    one = members[0, pl.ds(s, 1), :]
                    two = members[1, pl.ds(s, 1), :]
                    sums = jnp.where(sum_row == 0, one, jnp.where(sum_row == 1, two, 0.0))
                    chosen = jnp.concatenate([chosen, sums], axis=0)
                rows = jnp.dot(
                    chosen.astype(jnp.bfloat16), vec_ref[s], preferred_element_type=jnp.float32
                )
                packed[2 * s] = rows[:ROWS].astype(jnp.bfloat16)
                packed[2 * s + 1] = rows[ROWS : 2 * ROWS].astype(jnp.bfloat16)
                if c == 0:
                    count_one = jnp.sum(one, axis=1, keepdims=True)
                    count_two = jnp.sum(two, axis=1, keepdims=True)
                    cent_ref[pl.ds(2 * s, 1), :] = rows[2 * ROWS : 2 * ROWS + 1] / count_one
                    cent_ref[pl.ds(2 * s + 1, 1), :] = rows[2 * ROWS + 1 : 2 * ROWS + 2] / count_two
            return carry

        lax.fori_loop(0, s_local // GROUP, group, 0)

    def send(src, dst, send_sem, recv_sem, device):
        pltpu.make_async_remote_copy(
            src_ref=src, dst_ref=dst, send_sem=send_sem, recv_sem=recv_sem, device_id=device, device_id_type=MESH
        ).start()

    for c in range(chunks):
        pack_chunk(c)
        if c == 0:
            cent_own[...] = cent_ref[...].astype(jnp.bfloat16)
            pl.semaphore_wait(barrier, peers - 1 + n_rep - 1 + 1)
            send(cent_own, cent_in.at[turn], cent_sem, cent_in_sem.at[turn], post_id(relay))

        def fill_cross(i, carry):
            cross_send[c, i] = packed[cross_ref[i]]
            return carry

        lax.fori_loop(0, capacity, fill_cross, 0, unroll=4)
        send(
            cross_send.at[c],
            cross_in[c].at[turn, pl.ds(0, capacity)],
            cross_sem,
            cross_in_sem.at[c, turn],
            post_id(relay),
        )

        def fill_near(k, carry):
            at = (peer(k) - base) * hslot
            for i in range(hslot):
                near_send[c, k, i] = packed[near_ref[at + i]]
            return carry

        lax.fori_loop(0, peers, fill_near, 0)
        here = pl.ds(c * ROWS, ROWS)
        pltpu.make_async_copy(near_send.at[c, 0], out_ref.at[me, :, here, :], out_sem).start()

        def send_near(k, carry):
            send(near_send.at[c, k], out_ref.at[me, :, here, :], near_sem, out_sem, post_id(peer(k)))
            if c == 0:
                send(cent_own, cent_all.at[me], cent_sem, cent_all_sem, post_id(peer(k)))
            return carry

        lax.fori_loop(1, peers, send_near, 0)
        if c == 0:
            pltpu.make_async_copy(cent_own, cent_all.at[me], cent_all_sem).start()

    @pl.when(is_relay)
    def _():
        for j in range(2):
            wait_bytes(cent_in.at[j], cent_in_sem.at[j])
            origin = first_source + j * lanes
            pltpu.make_async_copy(cent_in.at[j], cent_all.at[origin], cent_all_sem).start()

            def forward_cent(k, carry):
                send(cent_in.at[j], cent_all.at[origin], cent_fwd_sem, cent_all_sem, post_id(peer(k)))
                return carry

            lax.fori_loop(1, peers, forward_cent, 0)

    def share_cents():
        wait_bytes(cent_all, cent_all_sem)
        for k in range(1, n_rep):
            send(cent_all, cent_rep.at[k - 1], rep_sem, rep_in_sem.at[k - 1], rep_id(k))

    def relay_chunk(c):
        for j in range(2):
            wait_bytes(cross_in[c].at[j, pl.ds(0, capacity)], cross_in_sem.at[c, j])
        here = pl.ds(c * ROWS, ROWS)
        for j in range(2):
            origin = first_source + j * lanes

            def fill(k, carry):
                at = (j * peers + peer(k) - base) * hslot
                for i in range(hslot):
                    relay_send[c, j, k, i] = cross_in[c][j, relay_ref[at + i]]
                return carry

            lax.fori_loop(0, peers, fill, 0)
            pltpu.make_async_copy(relay_send.at[c, j, 0], out_ref.at[origin, :, here, :], out_sem).start()

            def forward(k, carry):
                send(
                    relay_send.at[c, j, k],
                    out_ref.at[origin, :, here, :],
                    relay_sem,
                    out_sem,
                    post_id(peer(k)),
                )
                return carry

            lax.fori_loop(1, peers, forward, 0)

    for c in range(chunks):

        @pl.when(is_relay)
        def _():
            relay_chunk(c)

        if c == 1:
            share_cents()

    wait_bytes(cross_send, cross_sem)
    wait_bytes(near_send.at[:, pl.ds(1, peers - 1)], near_sem)
    wait_bytes(cent_all.at[pl.ds(0, peers)], cent_sem)
    wait_bytes(cent_rep, rep_sem)
    for k in range(1, n_rep):
        wait_bytes(cent_rep.at[k - 1], rep_in_sem.at[k - 1])

    @pl.when(is_relay)
    def _():
        wait_bytes(relay_send.at[:, :, pl.ds(1, peers - 1)], relay_sem)
        wait_bytes(cent_all.at[pl.ds(0, 2 * peers - 2)], cent_fwd_sem)

    wait_bytes(out_ref, out_sem)


def exchange(call_id, cross, near, relayed, vectors, labels, lengths, n_post, n_rep, hslot):
    s_local, length, dim_share = vectors.shape
    half_rows = length // 2
    n_halves = 2 * s_local
    capacity = cross.shape[0]
    peers = n_post // 2
    chunks = half_rows // ROWS
    bf16 = jnp.bfloat16
    in_smem = pl.BlockSpec(memory_space=pltpu.SMEM)
    in_vmem = pl.BlockSpec(memory_space=pltpu.VMEM)
    in_any = pl.BlockSpec(memory_space=pl.ANY)
    dma = pltpu.SemaphoreType.DMA
    return pl.pallas_call(
        exchange_kernel,
        in_specs=[in_smem] * 3 + [in_vmem] * 3,
        out_specs=[in_any, in_vmem, in_any, in_any],
        out_shape=[
            jax.ShapeDtypeStruct((n_post, hslot, half_rows, dim_share), bf16),
            jax.ShapeDtypeStruct((n_halves, dim_share), jnp.float32),
            jax.ShapeDtypeStruct((n_post, n_halves, dim_share), bf16),
            jax.ShapeDtypeStruct((n_rep - 1, n_post, n_halves, dim_share), bf16),
        ],
        scratch_shapes=[
            pltpu.VMEM((n_halves + 1, ROWS, dim_share), bf16),
            pltpu.VMEM((s_local, length), jnp.int32),
            pltpu.VMEM((2, s_local, length), jnp.float32),
            pltpu.VMEM((chunks, capacity, ROWS, dim_share), bf16),
            pltpu.VMEM((chunks, peers, hslot, ROWS, dim_share), bf16),
            pltpu.VMEM((chunks, 2, peers, hslot, ROWS, dim_share), bf16),
            pltpu.VMEM((n_halves, dim_share), bf16),
            pltpu.VMEM((2, n_halves, dim_share), bf16),
            dma,
            dma,
            dma,
            dma,
            dma,
            dma,
            dma((2,)),
            dma,
            dma,
            dma((n_rep - 1,)),
            dma((chunks, 2)),
        ]
        + [pltpu.VMEM((2, capacity + 1, ROWS, dim_share), bf16)] * chunks,
        compiler_params=pltpu.CompilerParams(
            collective_id=call_id, has_side_effects=True, vmem_limit_bytes=56 * 2**20
        ),
        cost_estimate=pl.CostEstimate(
            flops=4 * n_halves * half_rows * length * dim_share,
            bytes_accessed=2 * vectors.size + 4 * n_post * hslot * half_rows * dim_share,
            transcendentals=0,
        ),
    )(cross, near, relayed, vectors, labels, lengths[:, None])


def pick(mask, values, missing):
    found = jnp.sum(jnp.where(mask, values + 1, 0), axis=-1)
    return jnp.where(found > 0, found - 1, missing).astype(jnp.int32)


def routes(new_owners, n_post, hslot):
    n_halves = new_owners.size
    peers = n_post // 2
    lanes = n_post // 4
    me = lax.axis_index("post")
    owners = lax.all_gather(new_owners.reshape(1, -1), "post", axis=0, tiled=True)
    order = jnp.arange(n_halves)
    is_before = order[None, None, :] < order[None, :, None]
    same = (owners[:, :, None] == owners[:, None, :]) & is_before
    slot = jnp.sum(same.astype(jnp.int32), axis=2)
    crossing = owners // peers != (jnp.arange(n_post) // peers)[:, None]
    rank = jnp.sum((crossing[:, None, :] & is_before).astype(jnp.int32), axis=2)
    most = jnp.max(jnp.sum(crossing.astype(jnp.int32), axis=1))
    side = me // peers
    target = jnp.where(owners // peers == side, (owners - side * peers) * hslot + slot, -1)
    slots = jnp.arange(peers * hslot)
    sources = (1 - side) * peers + lax.rem(me, lanes) + jnp.arange(2) * lanes
    one = lambda array: lax.dynamic_index_in_dim(array, me, 0, keepdims=False)
    rank_mine = jnp.where(one(crossing), one(rank), -1)
    cross = pick(rank_mine[None, :] == order[:, None], order[None, :], n_halves)
    near = pick(one(target)[None, :] == slots[:, None], order[None, :], n_halves)
    relayed = pick(
        target[sources][:, None, :] == slots[None, :, None], rank[sources][:, None, :], n_halves
    )
    return cross, near, relayed.reshape(-1), most


def body(
    split_vectors,
    split_labels,
    split_lengths,
    new_owners,
    neighbour_ids,
    resident_vectors,
    resident_centroids,
    resident_lengths,
):
    n_post = lax.axis_size("post")
    s_local, length, dim_share = split_vectors.shape
    half_rows = length // 2
    hslot = max(2, 4 * s_local // n_post)
    res_local = resident_vectors.shape[0]
    n_rep = lax.axis_size("rep")
    res_part = res_local // n_rep
    post_index = lax.axis_index("post")
    rep_index = lax.axis_index("rep")
    mine_at = rep_index * res_part

    def shifted(array, offset):
        if offset == 0:
            return array
        return lax.ppermute(array, "rep", [(i, (i + offset) % n_rep) for i in range(n_rep)])

    def part_of(array, offset):
        at = lax.rem(rep_index + offset, n_rep) * res_part
        return lax.dynamic_slice_in_dim(array, at, res_part, 0)

    rows_shares = [shifted(part_of(resident_vectors, k), k) for k in range(n_rep)]
    current_shares = [shifted(part_of(resident_centroids, k), k) for k in range(n_rep)]

    cross, near, relayed, most = routes(new_owners, n_post, hslot)
    n_halves = 2 * s_local

    def with_room(call_id, capacity):
        return lambda: exchange(
            call_id,
            cross[:capacity],
            near,
            jnp.minimum(relayed, capacity),
            split_vectors,
            split_labels,
            split_lengths,
            n_post,
            n_rep,
            hslot,
        )

    usual = 5 * n_halves // 8
    new_postings, centroids, cent_mine, cent_rep = lax.cond(
        most <= usual, with_room(0, usual), with_room(1, n_halves)
    )
    new_centroids = centroids.reshape(s_local, 2, dim_share)
    n_cents = n_post * n_halves
    cent_shares = [cent_mine.reshape(n_cents, dim_share)]
    cent_shares += [cent_rep[k].reshape(n_cents, dim_share) for k in range(n_rep - 1)]
    my_postings = post_index * res_local + mine_at + jnp.arange(res_part)
    hits = jnp.any(neighbour_ids[:, :, None] == my_postings[None, None, :], axis=1)
    hits = jnp.repeat(hits, 2, axis=0).T

    own = 0.0
    row_norm = 0.0
    cent_norm = 0.0
    cross = 0.0
    for rows, current, cents in zip(rows_shares, current_shares, cent_shares):
        wide = rows.astype(jnp.float32)
        gap = wide - current.astype(jnp.float32)[:, None, :]
        own += jnp.sum(gap * gap, axis=2)
        row_norm += jnp.sum(wide * wide, axis=2)
        cents_wide = cents.astype(jnp.float32)
        cent_norm += jnp.sum(cents_wide * cents_wide, axis=1)
        cross += lax.dot_general(
            rows.reshape(res_part * length, dim_share),
            cents,
            (((1,), (1,)), ((), ())),
            preferred_element_type=jnp.float32,
        )
    distance = row_norm[:, :, None] - 2.0 * cross.reshape(res_part, length, n_cents) + cent_norm
    distance = jnp.where(hits[:, None, :], distance, far_value)
    best_dist = jnp.minimum(own, jnp.min(distance, axis=2))
    scores = (best_dist - row_norm) / math.sqrt(n_rep * dim_share)
    lengths_mine = part_of(resident_lengths, 0)
    scores = jnp.where(jnp.arange(length)[None, :] < lengths_mine[:, None], scores, 0.0)
    rescore = lax.all_gather(scores, "rep", axis=0, tiled=True)
    return (new_postings, new_centroids, rescore)


def solution(mesh):
    return jax.shard_map(
        body,
        mesh=mesh,
        in_specs=(
            P("post", None, "rep"),
            P("post", None),
            P("post"),
            P("post", None),
            P(),
            P("post", None, "rep"),
            P("post", "rep"),
            P("post"),
        ),
        out_specs=(P("post", None, None, "rep"), P("post", None, "rep"), P("post", None)),
        check_vma=False,
    )
```

```python
import functools
import math

import jax
import jax.numpy as jnp
from jax import lax
from jax.experimental import pallas as pl
from jax.experimental.pallas import tpu as pltpu
from jax.sharding import PartitionSpec as P

far_value = 1e30
ROWS = 16
GROUP = 4
MESH = pl.DeviceIdType.MESH


def wait_bytes(ref, sem):
    pltpu.make_async_copy(ref, ref, sem).wait()


def exchange_kernel(
    cross_ref,
    near_ref,
    relay_ref,
    vec_ref,
    label_ref,
    length_ref,
    nb_ref,
    res_ref,
    cur_ref,
    res_length_ref,
    out_ref,
    cent_ref,
    score_ref,
    cent_all,
    cent_rep,
    rows_in,
    cur_in,
    best,
    score_own,
    stage,
    packed,
    place,
    members,
    cross_send,
    near_send,
    relay_send,
    cent_own,
    cent_in,
    cross_sem,
    near_sem,
    relay_sem,
    out_sem,
    cent_sem,
    cent_fwd_sem,
    cent_in_sem,
    cent_all_sem,
    rep_sem,
    rep_in_sem,
    cross_in_sem,
    rows_sem,
    rows_in_sem,
    cur_sem,
    cur_in_sem,
    score_sem,
    score_in_sem,
    *cross_in,
):
    n_post = lax.axis_size("post")
    n_rep = lax.axis_size("rep")
    me = lax.axis_index("post")
    rep = lax.axis_index("rep")
    lanes = n_post // 4
    peers = n_post // 2
    side = me // peers
    base = side * peers
    layer = me // lanes
    lane = lax.rem(me, lanes)
    turn = lax.rem(layer, 2)
    relay = (2 - side) * lanes + lane
    is_relay = (layer == 1) | (layer == 2)
    first_source = (1 - side) * peers + lane
    s_local, length, dim_share = vec_ref.shape
    half_rows = length // 2
    n_halves = 2 * s_local
    hslot = out_ref.shape[1]
    capacity = cross_send.shape[1]
    chunks = half_rows // ROWS
    res_part = res_ref.shape[0] // n_rep

    def peer(k):
        return base + lax.rem(me - base + k, peers)

    def post_id(p):
        return {"post": p}

    def rep_id(k):
        return {"rep": lax.rem(rep + k, n_rep)}

    barrier = pltpu.get_barrier_semaphore()

    def greet(k, carry):
        pl.semaphore_signal(barrier, inc=1, device_id=post_id(peer(k)), device_id_type=MESH)
        return carry

    lax.fori_loop(1, peers, greet, 0)
    for k in range(1, n_rep):
        pl.semaphore_signal(barrier, inc=1, device_id=rep_id(k), device_id_type=MESH)

    @pl.when(is_relay)
    def _():
        for j in range(2):
            pl.semaphore_signal(
                barrier, inc=1, device_id=post_id(first_source + j * lanes), device_id_type=MESH
            )

    labels = label_ref[...]
    valid = lax.broadcasted_iota(jnp.int32, labels.shape, 1) < length_ref[...]
    first = jnp.where(valid & (labels == 0), 1.0, 0.0)
    second = jnp.where(valid & (labels == 1), 1.0, 0.0)
    earlier = lax.broadcasted_iota(jnp.int32, (length, length), 0) < lax.broadcasted_iota(
        jnp.int32, (length, length), 1
    )
    earlier = jnp.where(earlier, 1.0, 0.0).astype(jnp.bfloat16)
    rank_first = jnp.dot(first.astype(jnp.bfloat16), earlier, preferred_element_type=jnp.float32)
    rank_second = jnp.dot(second.astype(jnp.bfloat16), earlier, preferred_element_type=jnp.float32)
    spot = jnp.where(first > 0, rank_first, jnp.where(second > 0, half_rows + rank_second, -1.0))
    place[...] = spot.astype(jnp.int32)
    members[0] = first
    members[1] = second

    blank = jnp.zeros((ROWS, dim_share), jnp.bfloat16)
    packed[n_halves] = blank
    for c in range(chunks):
        for j in range(2):
            cross_in[c][j, capacity] = blank

    row = lax.broadcasted_iota(jnp.int32, (2 * ROWS, length), 0)
    row = jnp.where(row < ROWS, row, row - ROWS + half_rows)
    sum_row = lax.broadcasted_iota(jnp.int32, (ROWS, length), 0)

    def pack_chunk(c):
        def group(g, carry):
            for t in range(GROUP):
                s = g * GROUP + t
                chosen = jnp.where(row + c * ROWS == place[pl.ds(s, 1), :], 1.0, 0.0)
                if c == 0:
                    one = members[0, pl.ds(s, 1), :]
                    two = members[1, pl.ds(s, 1), :]
                    sums = jnp.where(sum_row == 0, one, jnp.where(sum_row == 1, two, 0.0))
                    chosen = jnp.concatenate([chosen, sums], axis=0)
                rows = jnp.dot(
                    chosen.astype(jnp.bfloat16), vec_ref[s], preferred_element_type=jnp.float32
                )
                packed[2 * s] = rows[:ROWS].astype(jnp.bfloat16)
                packed[2 * s + 1] = rows[ROWS : 2 * ROWS].astype(jnp.bfloat16)
                if c == 0:
                    count_one = jnp.sum(one, axis=1, keepdims=True)
                    count_two = jnp.sum(two, axis=1, keepdims=True)
                    cent_one = rows[2 * ROWS : 2 * ROWS + 1] / count_one
                    cent_two = rows[2 * ROWS + 1 : 2 * ROWS + 2] / count_two
                    cent_ref[pl.ds(2 * s, 1), :] = cent_one
                    cent_ref[pl.ds(2 * s + 1, 1), :] = cent_two
                    stage[pl.ds(s, 1), :] = cent_one
                    stage[pl.ds(s_local + s, 1), :] = cent_two
            return carry

        lax.fori_loop(0, s_local // GROUP, group, 0)

    def send(src, dst, send_sem, recv_sem, device):
        pltpu.make_async_remote_copy(
            src_ref=src, dst_ref=dst, send_sem=send_sem, recv_sem=recv_sem, device_id=device, device_id_type=MESH
        ).start()

    for c in range(chunks):
        pack_chunk(c)
        if c == 0:
            cent_own[...] = stage[...].astype(jnp.bfloat16)
            pl.semaphore_wait(barrier, peers - 1 + n_rep - 1 + 1)
            send(cent_own, cent_in.at[turn], cent_sem, cent_in_sem.at[turn], post_id(relay))

        def fill_cross(i, carry):
            cross_send[c, i] = packed[cross_ref[i]]
            return carry

        lax.fori_loop(0, capacity, fill_cross, 0, unroll=4)
        send(
            cross_send.at[c],
            cross_in[c].at[turn, pl.ds(0, capacity)],
            cross_sem,
            cross_in_sem.at[c, turn],
            post_id(relay),
        )

        def fill_near(k, carry):
            at = (peer(k) - base) * hslot
            for i in range(hslot):
                near_send[c, k, i] = packed[near_ref[at + i]]
            return carry

        lax.fori_loop(0, peers, fill_near, 0)
        here = pl.ds(c * ROWS, ROWS)
        pltpu.make_async_copy(near_send.at[c, 0], out_ref.at[me, :, here, :], out_sem).start()

        def send_near(k, carry):
            send(near_send.at[c, k], out_ref.at[me, :, here, :], near_sem, out_sem, post_id(peer(k)))
            if c == 0:
                send(cent_own, cent_all.at[me], cent_sem, cent_all_sem, post_id(peer(k)))
            return carry

        lax.fori_loop(1, peers, send_near, 0)
        if c == 0:
            pltpu.make_async_copy(cent_own, cent_all.at[me], cent_all_sem).start()
            for k in range(1, n_rep):
                theirs = pl.ds(lax.rem(rep + k, n_rep) * res_part, res_part)
                send(res_ref.at[theirs], rows_in.at[k - 1], rows_sem.at[k - 1], rows_in_sem.at[k - 1], rep_id(k))
                send(cur_ref, cur_in.at[k - 1], cur_sem.at[k - 1], cur_in_sem.at[k - 1], rep_id(k))

    @pl.when(is_relay)
    def _():
        for j in range(2):
            wait_bytes(cent_in.at[j], cent_in_sem.at[j])
            origin = first_source + j * lanes
            pltpu.make_async_copy(cent_in.at[j], cent_all.at[origin], cent_all_sem).start()

            def forward_cent(k, carry):
                send(cent_in.at[j], cent_all.at[origin], cent_fwd_sem, cent_all_sem, post_id(peer(k)))
                return carry

            lax.fori_loop(1, peers, forward_cent, 0)

    def share_cents():
        wait_bytes(cent_all, cent_all_sem)
        for k in range(1, n_rep):
            send(cent_all, cent_rep.at[k - 1], rep_sem, rep_in_sem.at[k - 1], rep_id(k))

    def rescore():
        for k in range(n_rep - 1):
            wait_bytes(cent_rep.at[k], rep_in_sem.at[k])
            wait_bytes(rows_in.at[k], rows_in_sem.at[k])
            wait_bytes(cur_in.at[k], cur_in_sem.at[k])
        first_mine = rep * res_part
        contract = (((1,), (1,)), ((), ()))

        def rows_of(k, q):
            return res_ref[first_mine + q] if k == 0 else rows_in[k - 1, q]

        def scores(vectors_of, count, q):
            norm = 0.0
            cross = 0.0
            for k in range(n_rep):
                vectors = vectors_of(k)
                wide = vectors.astype(jnp.float32)
                norm += jnp.sum(wide * wide, axis=1, keepdims=True)
                cross += lax.dot_general(
                    vectors, rows_of(k, q), contract, preferred_element_type=jnp.float32
                )
            return norm - 2.0 * cross

        postings = res_ref.shape[0]
        which = lax.broadcasted_iota(jnp.int32, (postings, length), 0)
        for q in range(res_part):
            own = scores(lambda k: cur_ref[...] if k == 0 else cur_in[k - 1], postings, q)
            own = jnp.where(which == first_mine + q, own, far_value)
            best[q : q + 1, :] = jnp.min(own, axis=0, keepdims=True)

        def group(g, carry):
            def cents_of(k):
                if k == 0:
                    block = cent_all[pl.ds(g * GROUP, GROUP)]
                else:
                    block = cent_rep[k - 1, pl.ds(g * GROUP, GROUP)]
                return block.reshape(GROUP * n_halves, dim_share)

            named = nb_ref[pl.ds(g * GROUP * s_local, GROUP * s_local), :]
            for q in range(res_part):
                posting = me * postings + first_mine + q
                hit = jnp.max(jnp.where(named == posting, 1.0, 0.0), axis=1, keepdims=True)
                hit = hit.reshape(GROUP, 1, s_local, 1)
                hit = jnp.concatenate([hit, hit], axis=1).reshape(GROUP * n_halves, 1)
                candidate = scores(cents_of, GROUP * n_halves, q)
                candidate = jnp.where(hit > 0.5, candidate, far_value)
                least = jnp.min(candidate, axis=0, keepdims=True)
                best[q : q + 1, :] = jnp.minimum(best[q : q + 1, :], least)
            return carry

        lax.fori_loop(0, n_post // GROUP, group, 0)
        lane_id = lax.broadcasted_iota(jnp.int32, (1, length), 1)
        for q in range(res_part):
            inside = lane_id < res_length_ref[first_mine + q]
            score = best[q : q + 1, :] * (1.0 / math.sqrt(n_rep * dim_share))
            score_own[q : q + 1, :] = jnp.where(inside, score, 0.0)
        score_ref[rep] = score_own[...]
        for k in range(1, n_rep):
            send(score_own, score_ref.at[rep], score_sem.at[k - 1], score_in_sem.at[k - 1], rep_id(k))

    def relay_chunk(c):
        for j in range(2):
            wait_bytes(cross_in[c].at[j, pl.ds(0, capacity)], cross_in_sem.at[c, j])
        here = pl.ds(c * ROWS, ROWS)
        for j in range(2):
            origin = first_source + j * lanes

            def fill(k, carry):
                at = (j * peers + peer(k) - base) * hslot
                for i in range(hslot):
                    relay_send[c, j, k, i] = cross_in[c][j, relay_ref[at + i]]
                return carry

            lax.fori_loop(0, peers, fill, 0)
            pltpu.make_async_copy(relay_send.at[c, j, 0], out_ref.at[origin, :, here, :], out_sem).start()

            def forward(k, carry):
                send(
                    relay_send.at[c, j, k],
                    out_ref.at[origin, :, here, :],
                    relay_sem,
                    out_sem,
                    post_id(peer(k)),
                )
                return carry

            lax.fori_loop(1, peers, forward, 0)

    for c in range(chunks):

        @pl.when(is_relay)
        def _():
            relay_chunk(c)

        if c == chunks // 2 - 1:
            share_cents()
        if c == chunks // 2:
            rescore()

    wait_bytes(cross_send, cross_sem)
    wait_bytes(near_send.at[:, pl.ds(1, peers - 1)], near_sem)
    wait_bytes(cent_all.at[pl.ds(0, peers)], cent_sem)
    wait_bytes(cent_rep, rep_sem)
    for k in range(n_rep - 1):
        wait_bytes(rows_in.at[k], rows_sem.at[k])
        wait_bytes(cur_in.at[k], cur_sem.at[k])
        wait_bytes(score_own, score_sem.at[k])
        wait_bytes(score_own, score_in_sem.at[k])

    @pl.when(is_relay)
    def _():
        wait_bytes(relay_send.at[:, :, pl.ds(1, peers - 1)], relay_sem)
        wait_bytes(cent_all.at[pl.ds(0, 2 * peers - 2)], cent_fwd_sem)

    wait_bytes(out_ref, out_sem)


def exchange(call_id, cross, near, relayed, vectors, labels, lengths, residents, n_post, n_rep, hslot):
    s_local, length, dim_share = vectors.shape
    half_rows = length // 2
    n_halves = 2 * s_local
    capacity = cross.shape[0]
    postings = residents[1].shape[0]
    res_part = postings // n_rep
    peers = n_post // 2
    chunks = half_rows // ROWS
    bf16 = jnp.bfloat16
    in_smem = pl.BlockSpec(memory_space=pltpu.SMEM)
    in_vmem = pl.BlockSpec(memory_space=pltpu.VMEM)
    in_any = pl.BlockSpec(memory_space=pl.ANY)
    dma = pltpu.SemaphoreType.DMA
    return pl.pallas_call(
        exchange_kernel,
        in_specs=[in_smem] * 3 + [in_vmem] * 6 + [in_smem],
        out_specs=[in_any, in_vmem, in_vmem],
        out_shape=[
            jax.ShapeDtypeStruct((n_post, hslot, half_rows, dim_share), bf16),
            jax.ShapeDtypeStruct((n_halves, dim_share), jnp.float32),
            jax.ShapeDtypeStruct((n_rep, res_part, length), jnp.float32),
        ],
        scratch_shapes=[
            pltpu.VMEM((n_post, n_halves, dim_share), bf16),
            pltpu.VMEM((n_rep - 1, n_post, n_halves, dim_share), bf16),
            pltpu.VMEM((n_rep - 1, res_part, length, dim_share), bf16),
            pltpu.VMEM((n_rep - 1, postings, dim_share), bf16),
            pltpu.VMEM((postings, length), jnp.float32),
            pltpu.VMEM((res_part, length), jnp.float32),
            pltpu.VMEM((n_halves, dim_share), jnp.float32),
            pltpu.VMEM((n_halves + 1, ROWS, dim_share), bf16),
            pltpu.VMEM((s_local, length), jnp.int32),
            pltpu.VMEM((2, s_local, length), jnp.float32),
            pltpu.VMEM((chunks, capacity, ROWS, dim_share), bf16),
            pltpu.VMEM((chunks, peers, hslot, ROWS, dim_share), bf16),
            pltpu.VMEM((chunks, 2, peers, hslot, ROWS, dim_share), bf16),
            pltpu.VMEM((n_halves, dim_share), bf16),
            pltpu.VMEM((2, n_halves, dim_share), bf16),
            dma,
            dma,
            dma,
            dma,
            dma,
            dma,
            dma((2,)),
            dma,
            dma,
            dma((n_rep - 1,)),
            dma((chunks, 2)),
        ]
        + [dma((n_rep - 1,))] * 6
        + [pltpu.VMEM((2, capacity + 1, ROWS, dim_share), bf16)] * chunks,
        compiler_params=pltpu.CompilerParams(
            collective_id=call_id, has_side_effects=True, vmem_limit_bytes=56 * 2**20
        ),
        cost_estimate=pl.CostEstimate(
            flops=4 * n_halves * half_rows * length * dim_share,
            bytes_accessed=2 * vectors.size + 4 * n_post * hslot * half_rows * dim_share,
            transcendentals=0,
        ),
    )(cross, near, relayed, vectors, labels, lengths[:, None], *residents)


def pick(mask, values, missing):
    found = jnp.sum(jnp.where(mask, values + 1, 0), axis=-1)
    return jnp.where(found > 0, found - 1, missing).astype(jnp.int32)


def routes(new_owners, n_post, hslot):
    n_halves = new_owners.size
    peers = n_post // 2
    lanes = n_post // 4
    me = lax.axis_index("post")
    owners = lax.all_gather(new_owners.reshape(1, -1), "post", axis=0, tiled=True)
    order = jnp.arange(n_halves)
    is_before = order[None, None, :] < order[None, :, None]
    same = (owners[:, :, None] == owners[:, None, :]) & is_before
    slot = jnp.sum(same.astype(jnp.int32), axis=2)
    crossing = owners // peers != (jnp.arange(n_post) // peers)[:, None]
    rank = jnp.sum((crossing[:, None, :] & is_before).astype(jnp.int32), axis=2)
    most = jnp.max(jnp.sum(crossing.astype(jnp.int32), axis=1))
    side = me // peers
    target = jnp.where(owners // peers == side, (owners - side * peers) * hslot + slot, -1)
    slots = jnp.arange(peers * hslot)
    sources = (1 - side) * peers + lax.rem(me, lanes) + jnp.arange(2) * lanes
    one = lambda array: lax.dynamic_index_in_dim(array, me, 0, keepdims=False)
    rank_mine = jnp.where(one(crossing), one(rank), -1)
    cross = pick(rank_mine[None, :] == order[:, None], order[None, :], n_halves)
    near = pick(one(target)[None, :] == slots[:, None], order[None, :], n_halves)
    relayed = pick(
        target[sources][:, None, :] == slots[None, :, None], rank[sources][:, None, :], n_halves
    )
    return cross, near, relayed.reshape(-1), most


def body(
    split_vectors,
    split_labels,
    split_lengths,
    new_owners,
    neighbour_ids,
    resident_vectors,
    resident_centroids,
    resident_lengths,
):
    n_post = lax.axis_size("post")
    s_local, length, dim_share = split_vectors.shape
    half_rows = length // 2
    hslot = max(2, 4 * s_local // n_post)
    n_rep = lax.axis_size("rep")
    cross, near, relayed, most = routes(new_owners, n_post, hslot)
    n_halves = 2 * s_local

    def with_room(call_id, capacity):
        return lambda: exchange(
            call_id,
            cross[:capacity],
            near,
            jnp.minimum(relayed, capacity),
            split_vectors,
            split_labels,
            split_lengths,
            (neighbour_ids, resident_vectors, resident_centroids, resident_lengths),
            n_post,
            n_rep,
            hslot,
        )

    usual = 5 * n_halves // 8
    new_postings, centroids, scores = lax.cond(
        most <= usual, with_room(0, usual), with_room(1, n_halves)
    )
    new_centroids = centroids.reshape(s_local, 2, dim_share)
    rescore = scores.reshape(resident_lengths.shape[0], length)
    return (new_postings, new_centroids, rescore)


def solution(mesh):
    return jax.shard_map(
        body,
        mesh=mesh,
        in_specs=(
            P("post", None, "rep"),
            P("post", None),
            P("post"),
            P("post", None),
            P(),
            P("post", None, "rep"),
            P("post", "rep"),
            P("post"),
        ),
        out_specs=(P("post", None, None, "rep"), P("post", None, "rep"), P("post", None)),
        check_vma=False,
    )
```

```python
import functools
import math

import jax
import jax.numpy as jnp
from jax import lax
from jax.experimental import pallas as pl
from jax.experimental.pallas import tpu as pltpu
from jax.sharding import PartitionSpec as P

far_value = 1e30
ROWS = 16
GROUP = 4
MESH = pl.DeviceIdType.MESH


def wait_bytes(ref, sem):
    pltpu.make_async_copy(ref, ref, sem).wait()


def exchange_kernel(
    cross_ref,
    near_ref,
    count_ref,
    res_length_ref,
    meta_ref,
    vec_ref,
    label_ref,
    length_ref,
    nb_ref,
    res_ref,
    cur_ref,
    out_ref,
    cent_ref,
    score_ref,
    most_ref,
    meta_in,
    meta,
    cent_all,
    cent_rep,
    rows_in,
    cur_in,
    best,
    score_own,
    stage,
    packed,
    place,
    members,
    cross_send,
    near_send,
    relay_send,
    cent_own,
    cent_in,
    cross_sem,
    near_sem,
    relay_sem,
    out_sem,
    cent_sem,
    cent_fwd_sem,
    cent_in_sem,
    cent_all_sem,
    rep_sem,
    rep_in_sem,
    cross_in_sem,
    rows_sem,
    rows_in_sem,
    cur_sem,
    cur_in_sem,
    score_sem,
    score_in_sem,
    meta_sem,
    meta_in_sem,
    meta_here_sem,
    *cross_in,
):
    n_post = lax.axis_size("post")
    n_rep = lax.axis_size("rep")
    me = lax.axis_index("post")
    rep = lax.axis_index("rep")
    lanes = n_post // 4
    peers = n_post // 2
    side = me // peers
    base = side * peers
    layer = me // lanes
    lane = lax.rem(me, lanes)
    turn = lax.rem(layer, 2)
    relay = (2 - side) * lanes + lane
    is_relay = (layer == 1) | (layer == 2)
    first_source = (1 - side) * peers + lane
    s_local, length, dim_share = vec_ref.shape
    half_rows = length // 2
    n_halves = 2 * s_local
    hslot = out_ref.shape[1]
    capacity = cross_send.shape[1]
    chunks = half_rows // ROWS
    res_part = res_ref.shape[0] // n_rep

    def peer(k):
        return base + lax.rem(me - base + k, peers)

    def post_id(p):
        return {"post": p}

    def rep_id(k):
        return {"rep": lax.rem(rep + k, n_rep)}

    barrier = pltpu.get_barrier_semaphore()

    def greet(k, carry):
        pl.semaphore_signal(barrier, inc=1, device_id=post_id(peer(k)), device_id_type=MESH)
        return carry

    lax.fori_loop(1, peers, greet, 0)
    for k in range(1, n_rep):
        pl.semaphore_signal(barrier, inc=1, device_id=rep_id(k), device_id_type=MESH)

    @pl.when(is_relay)
    def _():
        for j in range(2):
            pl.semaphore_signal(
                barrier, inc=1, device_id=post_id(first_source + j * lanes), device_id_type=MESH
            )

    labels = label_ref[...]
    valid = lax.broadcasted_iota(jnp.int32, labels.shape, 1) < length_ref[...]
    first = jnp.where(valid & (labels == 0), 1.0, 0.0)
    second = jnp.where(valid & (labels == 1), 1.0, 0.0)
    earlier = lax.broadcasted_iota(jnp.int32, (length, length), 0) < lax.broadcasted_iota(
        jnp.int32, (length, length), 1
    )
    earlier = jnp.where(earlier, 1.0, 0.0).astype(jnp.bfloat16)
    rank_first = jnp.dot(first.astype(jnp.bfloat16), earlier, preferred_element_type=jnp.float32)
    rank_second = jnp.dot(second.astype(jnp.bfloat16), earlier, preferred_element_type=jnp.float32)
    spot = jnp.where(first > 0, rank_first, jnp.where(second > 0, half_rows + rank_second, -1.0))
    place[...] = spot.astype(jnp.int32)
    members[0] = first
    members[1] = second

    blank = jnp.zeros((ROWS, dim_share), jnp.bfloat16)
    packed[n_halves] = blank
    for c in range(chunks):
        for j in range(2):
            cross_in[c][j, capacity] = blank

    row = lax.broadcasted_iota(jnp.int32, (2 * ROWS, length), 0)
    row = jnp.where(row < ROWS, row, row - ROWS + half_rows)
    sum_row = lax.broadcasted_iota(jnp.int32, (ROWS, length), 0)

    def pack_chunk(c):
        def group(g, carry):
            for t in range(GROUP):
                s = g * GROUP + t
                chosen = jnp.where(row + c * ROWS == place[pl.ds(s, 1), :], 1.0, 0.0)
                if c == 0:
                    one = members[0, pl.ds(s, 1), :]
                    two = members[1, pl.ds(s, 1), :]
                    sums = jnp.where(sum_row == 0, one, jnp.where(sum_row == 1, two, 0.0))
                    chosen = jnp.concatenate([chosen, sums], axis=0)
                rows = jnp.dot(
                    chosen.astype(jnp.bfloat16), vec_ref[s], preferred_element_type=jnp.float32
                )
                packed[2 * s] = rows[:ROWS].astype(jnp.bfloat16)
                packed[2 * s + 1] = rows[ROWS : 2 * ROWS].astype(jnp.bfloat16)
                if c == 0:
                    count_one = jnp.sum(one, axis=1, keepdims=True)
                    count_two = jnp.sum(two, axis=1, keepdims=True)
                    cent_one = rows[2 * ROWS : 2 * ROWS + 1] / count_one
                    cent_two = rows[2 * ROWS + 1 : 2 * ROWS + 2] / count_two
                    cent_ref[pl.ds(2 * s, 1), :] = cent_one
                    cent_ref[pl.ds(2 * s + 1, 1), :] = cent_two
                    stage[pl.ds(s, 1), :] = cent_one
                    stage[pl.ds(s_local + s, 1), :] = cent_two
            return carry

        lax.fori_loop(0, s_local // GROUP, group, 0)

    def send(src, dst, send_sem, recv_sem, device):
        pltpu.make_async_remote_copy(
            src_ref=src, dst_ref=dst, send_sem=send_sem, recv_sem=recv_sem, device_id=device, device_id_type=MESH
        ).start()

    for c in range(chunks):
        pack_chunk(c)
        if c == 0:
            cent_own[pl.ds(0, n_halves), :] = stage[...].astype(jnp.bfloat16)
            count = jnp.full((ROWS, dim_share), count_ref[0].astype(jnp.float32), jnp.float32)
            cent_own[pl.ds(n_halves, ROWS), :] = count.astype(jnp.bfloat16)
            pl.semaphore_wait(barrier, peers - 1 + n_rep - 1 + 1)
            send(meta_ref, meta_in.at[turn], meta_sem, meta_in_sem.at[turn], post_id(relay))
            send(cent_own, cent_in.at[turn], cent_sem, cent_in_sem.at[turn], post_id(relay))

        def fill_cross(i, carry):
            cross_send[c, i] = packed[cross_ref[i]]
            return carry

        lax.fori_loop(0, capacity, fill_cross, 0, unroll=2)
        send(
            cross_send.at[c],
            cross_in[c].at[turn, pl.ds(0, capacity)],
            cross_sem,
            cross_in_sem.at[c, turn],
            post_id(relay),
        )

        def fill_near(k, carry):
            at = (peer(k) - base) * hslot
            for i in range(hslot):
                near_send[c, k, i] = packed[near_ref[at + i]]
            return carry

        lax.fori_loop(0, peers, fill_near, 0)
        here = pl.ds(c * ROWS, ROWS)
        pltpu.make_async_copy(near_send.at[c, 0], out_ref.at[me, :, here, :], out_sem).start()

        def send_near(k, carry):
            send(near_send.at[c, k], out_ref.at[me, :, here, :], near_sem, out_sem, post_id(peer(k)))
            if c == 0:
                send(cent_own, cent_all.at[me], cent_sem, cent_all_sem, post_id(peer(k)))
            return carry

        lax.fori_loop(1, peers, send_near, 0)
        if c == 0:
            pltpu.make_async_copy(cent_own, cent_all.at[me], cent_all_sem).start()
            for k in range(1, n_rep):
                theirs = pl.ds(lax.rem(rep + k, n_rep) * res_part, res_part)
                send(res_ref.at[theirs], rows_in.at[k - 1], rows_sem.at[k - 1], rows_in_sem.at[k - 1], rep_id(k))
                send(cur_ref, cur_in.at[k - 1], cur_sem.at[k - 1], cur_in_sem.at[k - 1], rep_id(k))

    @pl.when(is_relay)
    def _():
        for j in range(2):
            wait_bytes(meta_in.at[j], meta_in_sem.at[j])
            pltpu.make_async_copy(meta_in.at[j], meta.at[j], meta_here_sem.at[j]).start()
        for j in range(2):
            wait_bytes(meta.at[j], meta_here_sem.at[j])
        for j in range(2):
            wait_bytes(cent_in.at[j], cent_in_sem.at[j])
            origin = first_source + j * lanes
            pltpu.make_async_copy(cent_in.at[j], cent_all.at[origin], cent_all_sem).start()

            def forward_cent(k, carry):
                send(cent_in.at[j], cent_all.at[origin], cent_fwd_sem, cent_all_sem, post_id(peer(k)))
                return carry

            lax.fori_loop(1, peers, forward_cent, 0)

    def share_cents():
        wait_bytes(cent_all, cent_all_sem)
        counts = cent_all[:, pl.ds(n_halves, ROWS), pl.ds(0, 128)].astype(jnp.float32)
        most_ref[...] = jnp.max(counts, axis=0)
        for k in range(1, n_rep):
            send(cent_all, cent_rep.at[k - 1], rep_sem, rep_in_sem.at[k - 1], rep_id(k))

    def rescore():
        for k in range(n_rep - 1):
            wait_bytes(cent_rep.at[k], rep_in_sem.at[k])
            wait_bytes(rows_in.at[k], rows_in_sem.at[k])
            wait_bytes(cur_in.at[k], cur_in_sem.at[k])
        first_mine = rep * res_part
        contract = (((1,), (1,)), ((), ()))

        def rows_of(k, q):
            return res_ref[first_mine + q] if k == 0 else rows_in[k - 1, q]

        def scores(vectors_of, count, q):
            norm = 0.0
            cross = 0.0
            for k in range(n_rep):
                vectors = vectors_of(k)
                wide = vectors.astype(jnp.float32)
                norm += jnp.sum(wide * wide, axis=1, keepdims=True)
                cross += lax.dot_general(
                    vectors, rows_of(k, q), contract, preferred_element_type=jnp.float32
                )
            return norm - 2.0 * cross

        postings = res_ref.shape[0]
        which = lax.broadcasted_iota(jnp.int32, (postings, length), 0)
        for q in range(res_part):
            own = scores(lambda k: cur_ref[...] if k == 0 else cur_in[k - 1], postings, q)
            own = jnp.where(which == first_mine + q, own, far_value)
            best[q : q + 1, :] = jnp.min(own, axis=0, keepdims=True)

        def group(g, carry):
            def cents_of(k):
                if k == 0:
                    block = cent_all[pl.ds(g * GROUP, GROUP), pl.ds(0, n_halves)]
                else:
                    block = cent_rep[k - 1, pl.ds(g * GROUP, GROUP), pl.ds(0, n_halves)]
                return block.reshape(GROUP * n_halves, dim_share)

            named = nb_ref[pl.ds(g * GROUP * s_local, GROUP * s_local), :]
            for q in range(res_part):
                posting = me * postings + first_mine + q
                hit = jnp.max(jnp.where(named == posting, 1.0, 0.0), axis=1, keepdims=True)
                hit = hit.reshape(GROUP, 1, s_local, 1)
                hit = jnp.concatenate([hit, hit], axis=1).reshape(GROUP * n_halves, 1)
                candidate = scores(cents_of, GROUP * n_halves, q)
                candidate = jnp.where(hit > 0.5, candidate, far_value)
                least = jnp.min(candidate, axis=0, keepdims=True)
                best[q : q + 1, :] = jnp.minimum(best[q : q + 1, :], least)
            return carry

        lax.fori_loop(0, n_post // GROUP, group, 0)
        lane_id = lax.broadcasted_iota(jnp.int32, (1, length), 1)
        for q in range(res_part):
            inside = lane_id < res_length_ref[first_mine + q]
            score = best[q : q + 1, :] * (1.0 / math.sqrt(n_rep * dim_share))
            score_own[q : q + 1, :] = jnp.where(inside, score, 0.0)
        score_ref[rep] = score_own[...]
        for k in range(1, n_rep):
            send(score_own, score_ref.at[rep], score_sem.at[k - 1], score_in_sem.at[k - 1], rep_id(k))

    def relay_chunk(c):
        for j in range(2):
            wait_bytes(cross_in[c].at[j, pl.ds(0, capacity)], cross_in_sem.at[c, j])
        here = pl.ds(c * ROWS, ROWS)
        for j in range(2):
            origin = first_source + j * lanes

            def fill(k, carry):
                at = (peer(k) - base) * hslot
                for i in range(hslot):
                    relay_send[c, j, k, i] = cross_in[c][j, meta[j, 0, at + i]]
                return carry

            lax.fori_loop(0, peers, fill, 0)
            pltpu.make_async_copy(relay_send.at[c, j, 0], out_ref.at[origin, :, here, :], out_sem).start()

            def forward(k, carry):
                send(
                    relay_send.at[c, j, k],
                    out_ref.at[origin, :, here, :],
                    relay_sem,
                    out_sem,
                    post_id(peer(k)),
                )
                return carry

            lax.fori_loop(1, peers, forward, 0)

    for c in range(chunks):

        @pl.when(is_relay)
        def _():
            relay_chunk(c)

        if c == chunks // 2 - 1:
            share_cents()
        if c == chunks // 2:
            rescore()

    wait_bytes(meta_ref, meta_sem)
    wait_bytes(cross_send, cross_sem)
    wait_bytes(near_send.at[:, pl.ds(1, peers - 1)], near_sem)
    wait_bytes(cent_all.at[pl.ds(0, peers)], cent_sem)
    wait_bytes(cent_rep, rep_sem)
    for k in range(n_rep - 1):
        wait_bytes(rows_in.at[k], rows_sem.at[k])
        wait_bytes(cur_in.at[k], cur_sem.at[k])
        wait_bytes(score_own, score_sem.at[k])
        wait_bytes(score_own, score_in_sem.at[k])

    @pl.when(is_relay)
    def _():
        wait_bytes(relay_send.at[:, :, pl.ds(1, peers - 1)], relay_sem)
        wait_bytes(cent_all.at[pl.ds(0, 2 * peers - 2)], cent_fwd_sem)

    wait_bytes(out_ref, out_sem)


def exchange(call_id, cross, near, count, meta, vectors, labels, lengths, residents, n_post, n_rep, hslot):
    neighbour_ids, res_vectors, res_centroids, res_lengths = residents
    s_local, length, dim_share = vectors.shape
    half_rows = length // 2
    n_halves = 2 * s_local
    capacity = cross.shape[0]
    postings = res_vectors.shape[0]
    res_part = postings // n_rep
    peers = n_post // 2
    chunks = half_rows // ROWS
    bf16 = jnp.bfloat16
    in_smem = pl.BlockSpec(memory_space=pltpu.SMEM)
    in_vmem = pl.BlockSpec(memory_space=pltpu.VMEM)
    in_any = pl.BlockSpec(memory_space=pl.ANY)
    dma = pltpu.SemaphoreType.DMA
    return pl.pallas_call(
        exchange_kernel,
        in_specs=[in_smem] * 4 + [in_vmem] * 7,
        out_specs=[in_any, in_vmem, in_vmem, in_vmem],
        out_shape=[
            jax.ShapeDtypeStruct((n_post, hslot, half_rows, dim_share), bf16),
            jax.ShapeDtypeStruct((n_halves, dim_share), jnp.float32),
            jax.ShapeDtypeStruct((n_rep, res_part, length), jnp.float32),
            jax.ShapeDtypeStruct((ROWS, 128), jnp.float32),
        ],
        scratch_shapes=[
            pltpu.VMEM((2,) + meta.shape, jnp.int32),
            pltpu.SMEM((2,) + meta.shape, jnp.int32),
            pltpu.VMEM((n_post, n_halves + ROWS, dim_share), bf16),
            pltpu.VMEM((n_rep - 1, n_post, n_halves + ROWS, dim_share), bf16),
            pltpu.VMEM((n_rep - 1, res_part, length, dim_share), bf16),
            pltpu.VMEM((n_rep - 1, postings, dim_share), bf16),
            pltpu.VMEM((postings, length), jnp.float32),
            pltpu.VMEM((res_part, length), jnp.float32),
            pltpu.VMEM((n_halves, dim_share), jnp.float32),
            pltpu.VMEM((n_halves + 1, ROWS, dim_share), bf16),
            pltpu.VMEM((s_local, length), jnp.int32),
            pltpu.VMEM((2, s_local, length), jnp.float32),
            pltpu.VMEM((chunks, capacity, ROWS, dim_share), bf16),
            pltpu.VMEM((chunks, peers, hslot, ROWS, dim_share), bf16),
            pltpu.VMEM((chunks, 2, peers, hslot, ROWS, dim_share), bf16),
            pltpu.VMEM((n_halves + ROWS, dim_share), bf16),
            pltpu.VMEM((2, n_halves + ROWS, dim_share), bf16),
            dma,
            dma,
            dma,
            dma,
            dma,
            dma,
            dma((2,)),
            dma,
            dma,
            dma((n_rep - 1,)),
            dma((chunks, 2)),
        ]
        + [dma((n_rep - 1,))] * 6
        + [dma, dma((2,)), dma((2,))]
        + [pltpu.VMEM((2, capacity + 1, ROWS, dim_share), bf16)] * chunks,
        compiler_params=pltpu.CompilerParams(
            collective_id=call_id, has_side_effects=True, vmem_limit_bytes=56 * 2**20
        ),
        cost_estimate=pl.CostEstimate(
            flops=4 * n_halves * half_rows * length * dim_share,
            bytes_accessed=2 * vectors.size + 4 * n_post * hslot * half_rows * dim_share,
            transcendentals=0,
        ),
    )(
        cross,
        near,
        count,
        res_lengths,
        meta,
        vectors,
        labels,
        lengths[:, None],
        neighbour_ids,
        res_vectors,
        res_centroids,
    )


def move_kernel(src_ref, dst_ref, room, in_sem, out_sem):
    blocks = src_ref.shape[0]
    for i in range(blocks):
        pltpu.make_async_copy(src_ref.at[i], room.at[i], in_sem.at[i]).start()
    for i in range(blocks):
        pltpu.make_async_copy(src_ref.at[i], room.at[i], in_sem.at[i]).wait()
        pltpu.make_async_copy(room.at[i], dst_ref.at[i], out_sem.at[i]).start()
    for i in range(blocks):
        pltpu.make_async_copy(room.at[i], dst_ref.at[i], out_sem.at[i]).wait()


def move(array):
    return pl.pallas_call(
        move_kernel,
        in_specs=[pl.BlockSpec(memory_space=pl.ANY)],
        out_specs=pl.BlockSpec(memory_space=pl.ANY),
        out_shape=jax.ShapeDtypeStruct(array.shape, array.dtype),
        scratch_shapes=[
            pltpu.VMEM(array.shape, array.dtype),
            pltpu.SemaphoreType.DMA((array.shape[0],)),
            pltpu.SemaphoreType.DMA((array.shape[0],)),
        ],
        compiler_params=pltpu.CompilerParams(vmem_limit_bytes=40 * 2**20),
    )(array)


def pick(mask, values, missing):
    found = jnp.sum(jnp.where(mask, values + 1, 0), axis=-1)
    return jnp.where(found > 0, found - 1, missing).astype(jnp.int32)


def routes(new_owners, n_post, hslot):
    n_halves = new_owners.size
    peers = n_post // 2
    side = lax.axis_index("post") // peers
    owner = new_owners.reshape(-1)
    order = jnp.arange(n_halves)
    is_before = order[None, :] < order[:, None]
    slot = jnp.sum(((owner[:, None] == owner[None, :]) & is_before).astype(jnp.int32), axis=1)
    crossing = owner // peers != side
    rank = jnp.sum((crossing[None, :] & is_before).astype(jnp.int32), axis=1)
    target = owner * hslot + slot
    slots = jnp.arange(peers * hslot)
    cross = pick(jnp.where(crossing, rank, -1)[None, :] == order[:, None], order[None, :], n_halves)
    near = pick(target[None, :] == side * peers * hslot + slots[:, None], order[None, :], n_halves)
    meta = pick(target[None, :] == (1 - side) * peers * hslot + slots[:, None], rank[None, :], n_halves)
    count = jnp.sum(crossing.astype(jnp.int32)).reshape(1)
    return cross, near, meta, count


def body(
    split_vectors,
    split_labels,
    split_lengths,
    new_owners,
    neighbour_ids,
    resident_vectors,
    resident_centroids,
    resident_lengths,
):
    n_post = lax.axis_size("post")
    s_local, length, dim_share = split_vectors.shape
    half_rows = length // 2
    hslot = max(2, 4 * s_local // n_post)
    n_rep = lax.axis_size("rep")
    cross, near, meta, count = routes(new_owners, n_post, hslot)
    n_halves = 2 * s_local

    def with_room(call_id, capacity):
        table = jnp.minimum(meta, capacity)
        table = jnp.broadcast_to(jnp.pad(table, (0, -table.size % 128))[None, :], (8, table.size + -table.size % 128))
        return exchange(
            call_id,
            cross[:capacity],
            near,
            count,
            table,
            split_vectors,
            split_labels,
            split_lengths,
            (neighbour_ids, resident_vectors, resident_centroids, resident_lengths),
            n_post,
            n_rep,
            hslot,
        )

    usual = 23 * n_halves // 32
    stored, centroids, scores, most = with_room(0, usual)
    stored, _ = lax.while_loop(
        lambda state: state[1] > usual,
        lambda state: (with_room(1, n_halves)[0], jnp.float32(0)),
        (stored, most[0, 0]),
    )
    new_postings = move(stored)
    new_centroids = centroids.reshape(s_local, 2, dim_share)
    rescore = scores.reshape(resident_lengths.shape[0], length)
    return (new_postings, new_centroids, rescore)


def solution(mesh):
    return jax.shard_map(
        body,
        mesh=mesh,
        in_specs=(
            P("post", None, "rep"),
            P("post", None),
            P("post"),
            P("post", None),
            P(),
            P("post", None, "rep"),
            P("post", "rep"),
            P("post"),
        ),
        out_specs=(P("post", None, None, "rep"), P("post", None, "rep"), P("post", None)),
        check_vma=False,
    )
```

```python
import functools
import math

import jax
import jax.numpy as jnp
from jax import lax
from jax.experimental import pallas as pl
from jax.experimental.pallas import tpu as pltpu
from jax.sharding import PartitionSpec as P

far_value = 1e30
ROWS = 16
SPANS = 2
GROUP = 4
MESH = pl.DeviceIdType.MESH


def wait_bytes(ref, sem):
    pltpu.make_async_copy(ref, ref, sem).wait()


def exchange_kernel(
    cross_ref,
    near_ref,
    count_ref,
    res_length_ref,
    meta_ref,
    vec_ref,
    label_ref,
    length_ref,
    nb_ref,
    res_ref,
    cur_ref,
    out_ref,
    cent_ref,
    score_ref,
    most_ref,
    meta_in,
    meta,
    cent_all,
    cent_rep,
    rows_in,
    cur_in,
    best,
    score_own,
    stage,
    packed,
    place,
    members,
    cross_send,
    near_send,
    relay_send,
    cent_own,
    cent_in,
    cross_sem,
    near_sem,
    relay_sem,
    out_sem,
    cent_sem,
    cent_fwd_sem,
    cent_in_sem,
    cent_all_sem,
    rep_sem,
    rep_in_sem,
    cross_in_sem,
    rows_sem,
    rows_in_sem,
    cur_sem,
    cur_in_sem,
    score_sem,
    score_in_sem,
    meta_sem,
    meta_in_sem,
    meta_here_sem,
    *cross_in,
):
    n_post = lax.axis_size("post")
    n_rep = lax.axis_size("rep")
    me = lax.axis_index("post")
    rep = lax.axis_index("rep")
    lanes = n_post // 4
    peers = n_post // 2
    side = me // peers
    base = side * peers
    layer = me // lanes
    lane = lax.rem(me, lanes)
    turn = lax.rem(layer, 2)
    relay = (2 - side) * lanes + lane
    is_relay = (layer == 1) | (layer == 2)
    first_source = (1 - side) * peers + lane
    s_local, length, dim_share = vec_ref.shape
    half_rows = length // 2
    n_halves = 2 * s_local
    hslot = out_ref.shape[1]
    capacity = cross_send.shape[1]
    chunks = half_rows // ROWS
    res_part = res_ref.shape[0] // n_rep
    width = dim_share // SPANS

    def peer(k):
        return base + lax.rem(me - base + k, peers)

    def post_id(p):
        return {"post": p}

    def rep_id(k):
        return {"rep": lax.rem(rep + k, n_rep)}

    barrier = pltpu.get_barrier_semaphore()

    def greet(k, carry):
        pl.semaphore_signal(barrier, inc=1, device_id=post_id(peer(k)), device_id_type=MESH)
        return carry

    lax.fori_loop(1, peers, greet, 0)
    for k in range(1, n_rep):
        pl.semaphore_signal(barrier, inc=1, device_id=rep_id(k), device_id_type=MESH)

    @pl.when(is_relay)
    def _():
        for j in range(2):
            pl.semaphore_signal(
                barrier, inc=1, device_id=post_id(first_source + j * lanes), device_id_type=MESH
            )

    labels = label_ref[...]
    valid = lax.broadcasted_iota(jnp.int32, labels.shape, 1) < length_ref[...]
    first = jnp.where(valid & (labels == 0), 1.0, 0.0)
    second = jnp.where(valid & (labels == 1), 1.0, 0.0)
    earlier = lax.broadcasted_iota(jnp.int32, (length, length), 0) < lax.broadcasted_iota(
        jnp.int32, (length, length), 1
    )
    earlier = jnp.where(earlier, 1.0, 0.0).astype(jnp.bfloat16)
    rank_first = jnp.dot(first.astype(jnp.bfloat16), earlier, preferred_element_type=jnp.float32)
    rank_second = jnp.dot(second.astype(jnp.bfloat16), earlier, preferred_element_type=jnp.float32)
    spot = jnp.where(first > 0, rank_first, jnp.where(second > 0, half_rows + rank_second, -1.0))
    place[...] = spot.astype(jnp.int32)
    members[0] = first
    members[1] = second

    blank = jnp.zeros((ROWS, dim_share), jnp.bfloat16)
    packed[n_halves] = blank
    for u in range(chunks * SPANS):
        for j in range(2):
            cross_in[u][j, capacity] = blank[:, :width]

    row = lax.broadcasted_iota(jnp.int32, (2 * ROWS, length), 0)
    row = jnp.where(row < ROWS, row, row - ROWS + half_rows)
    sum_row = lax.broadcasted_iota(jnp.int32, (ROWS, length), 0)

    def pack_chunk(c):
        def group(g, carry):
            for t in range(GROUP):
                s = g * GROUP + t
                chosen = jnp.where(row + c * ROWS == place[pl.ds(s, 1), :], 1.0, 0.0)
                if c == 0:
                    one = members[0, pl.ds(s, 1), :]
                    two = members[1, pl.ds(s, 1), :]
                    sums = jnp.where(sum_row == 0, one, jnp.where(sum_row == 1, two, 0.0))
                    chosen = jnp.concatenate([chosen, sums], axis=0)
                rows = jnp.dot(
                    chosen.astype(jnp.bfloat16), vec_ref[s], preferred_element_type=jnp.float32
                )
                packed[2 * s] = rows[:ROWS].astype(jnp.bfloat16)
                packed[2 * s + 1] = rows[ROWS : 2 * ROWS].astype(jnp.bfloat16)
                if c == 0:
                    count_one = jnp.sum(one, axis=1, keepdims=True)
                    count_two = jnp.sum(two, axis=1, keepdims=True)
                    cent_one = rows[2 * ROWS : 2 * ROWS + 1] / count_one
                    cent_two = rows[2 * ROWS + 1 : 2 * ROWS + 2] / count_two
                    cent_ref[pl.ds(2 * s, 1), :] = cent_one
                    cent_ref[pl.ds(2 * s + 1, 1), :] = cent_two
                    stage[pl.ds(s, 1), :] = cent_one
                    stage[pl.ds(s_local + s, 1), :] = cent_two
            return carry

        lax.fori_loop(0, s_local // GROUP, group, 0)

    def send(src, dst, send_sem, recv_sem, device):
        pltpu.make_async_remote_copy(
            src_ref=src, dst_ref=dst, send_sem=send_sem, recv_sem=recv_sem, device_id=device, device_id_type=MESH
        ).start()

    for c in range(chunks):
        pack_chunk(c)
        if c == 0:
            cent_own[pl.ds(0, n_halves), :] = stage[...].astype(jnp.bfloat16)
            count = jnp.full((ROWS, dim_share), count_ref[0].astype(jnp.float32), jnp.float32)
            cent_own[pl.ds(n_halves, ROWS), :] = count.astype(jnp.bfloat16)
            pl.semaphore_wait(barrier, peers - 1 + n_rep - 1 + 1)
            send(meta_ref, meta_in.at[turn], meta_sem, meta_in_sem.at[turn], post_id(relay))
            send(cent_own, cent_in.at[turn], cent_sem, cent_in_sem.at[turn], post_id(relay))

        def fill_cross(i, carry):
            rows = packed[cross_ref[i]]
            for b in range(SPANS):
                cross_send[c * SPANS + b, i] = rows[:, b * width : (b + 1) * width]
            return carry

        lax.fori_loop(0, capacity, fill_cross, 0)
        for u in range(c * SPANS, (c + 1) * SPANS):
            send(
                cross_send.at[u],
                cross_in[u].at[turn, pl.ds(0, capacity)],
                cross_sem,
                cross_in_sem.at[u, turn],
                post_id(relay),
            )

        def fill_near(k, carry):
            at = (peer(k) - base) * hslot
            for i in range(hslot):
                near_send[c, k, i] = packed[near_ref[at + i]]
            return carry

        lax.fori_loop(0, peers, fill_near, 0)
        here = pl.ds(c * ROWS, ROWS)
        pltpu.make_async_copy(near_send.at[c, 0], out_ref.at[me, :, here, :], out_sem).start()

        def send_near(k, carry):
            send(near_send.at[c, k], out_ref.at[me, :, here, :], near_sem, out_sem, post_id(peer(k)))
            if c == 0:
                send(cent_own, cent_all.at[me], cent_sem, cent_all_sem, post_id(peer(k)))
            return carry

        lax.fori_loop(1, peers, send_near, 0)
        if c == 0:
            pltpu.make_async_copy(cent_own, cent_all.at[me], cent_all_sem).start()
            for k in range(1, n_rep):
                theirs = pl.ds(lax.rem(rep + k, n_rep) * res_part, res_part)
                send(res_ref.at[theirs], rows_in.at[k - 1], rows_sem.at[k - 1], rows_in_sem.at[k - 1], rep_id(k))
                send(cur_ref, cur_in.at[k - 1], cur_sem.at[k - 1], cur_in_sem.at[k - 1], rep_id(k))

    @pl.when(is_relay)
    def _():
        for j in range(2):
            wait_bytes(meta_in.at[j], meta_in_sem.at[j])
            pltpu.make_async_copy(meta_in.at[j], meta.at[j], meta_here_sem.at[j]).start()
        for j in range(2):
            wait_bytes(meta.at[j], meta_here_sem.at[j])
        for j in range(2):
            wait_bytes(cent_in.at[j], cent_in_sem.at[j])
            origin = first_source + j * lanes
            pltpu.make_async_copy(cent_in.at[j], cent_all.at[origin], cent_all_sem).start()

            def forward_cent(k, carry):
                send(cent_in.at[j], cent_all.at[origin], cent_fwd_sem, cent_all_sem, post_id(peer(k)))
                return carry

            lax.fori_loop(1, peers, forward_cent, 0)

    def share_cents():
        wait_bytes(cent_all, cent_all_sem)
        counts = cent_all[:, pl.ds(n_halves, ROWS), pl.ds(0, 128)].astype(jnp.float32)
        most_ref[...] = jnp.max(counts, axis=0)
        for k in range(1, n_rep):
            send(cent_all, cent_rep.at[k - 1], rep_sem, rep_in_sem.at[k - 1], rep_id(k))

    def rescore():
        for k in range(n_rep - 1):
            wait_bytes(cent_rep.at[k], rep_in_sem.at[k])
            wait_bytes(rows_in.at[k], rows_in_sem.at[k])
            wait_bytes(cur_in.at[k], cur_in_sem.at[k])
        first_mine = rep * res_part
        contract = (((1,), (1,)), ((), ()))

        def rows_of(k, q):
            return res_ref[first_mine + q] if k == 0 else rows_in[k - 1, q]

        def scores(vectors_of, count, q):
            norm = 0.0
            cross = 0.0
            for k in range(n_rep):
                vectors = vectors_of(k)
                wide = vectors.astype(jnp.float32)
                norm += jnp.sum(wide * wide, axis=1, keepdims=True)
                cross += lax.dot_general(
                    vectors, rows_of(k, q), contract, preferred_element_type=jnp.float32
                )
            return norm - 2.0 * cross

        postings = res_ref.shape[0]
        which = lax.broadcasted_iota(jnp.int32, (postings, length), 0)
        for q in range(res_part):
            own = scores(lambda k: cur_ref[...] if k == 0 else cur_in[k - 1], postings, q)
            own = jnp.where(which == first_mine + q, own, far_value)
            best[q : q + 1, :] = jnp.min(own, axis=0, keepdims=True)

        def group(g, carry):
            def cents_of(k):
                if k == 0:
                    block = cent_all[pl.ds(g * GROUP, GROUP), pl.ds(0, n_halves)]
                else:
                    block = cent_rep[k - 1, pl.ds(g * GROUP, GROUP), pl.ds(0, n_halves)]
                return block.reshape(GROUP * n_halves, dim_share)

            named = nb_ref[pl.ds(g * GROUP * s_local, GROUP * s_local), :]
            for q in range(res_part):
                posting = me * postings + first_mine + q
                hit = jnp.max(jnp.where(named == posting, 1.0, 0.0), axis=1, keepdims=True)
                hit = hit.reshape(GROUP, 1, s_local, 1)
                hit = jnp.concatenate([hit, hit], axis=1).reshape(GROUP * n_halves, 1)
                candidate = scores(cents_of, GROUP * n_halves, q)
                candidate = jnp.where(hit > 0.5, candidate, far_value)
                least = jnp.min(candidate, axis=0, keepdims=True)
                best[q : q + 1, :] = jnp.minimum(best[q : q + 1, :], least)
            return carry

        lax.fori_loop(0, n_post // GROUP, group, 0)
        lane_id = lax.broadcasted_iota(jnp.int32, (1, length), 1)
        for q in range(res_part):
            inside = lane_id < res_length_ref[first_mine + q]
            score = best[q : q + 1, :] * (1.0 / math.sqrt(n_rep * dim_share))
            score_own[q : q + 1, :] = jnp.where(inside, score, 0.0)
        score_ref[rep] = score_own[...]
        for k in range(1, n_rep):
            send(score_own, score_ref.at[rep], score_sem.at[k - 1], score_in_sem.at[k - 1], rep_id(k))

    def relay_chunk(u):
        for j in range(2):
            wait_bytes(cross_in[u].at[j, pl.ds(0, capacity)], cross_in_sem.at[u, j])
        here = pl.ds(u // SPANS * ROWS, ROWS)
        cols = pl.ds(u % SPANS * width, width)
        for j in range(2):
            origin = first_source + j * lanes

            def fill(k, carry):
                at = (peer(k) - base) * hslot
                for i in range(hslot):
                    relay_send[u, j, k, i] = cross_in[u][j, meta[j, 0, at + i]]
                return carry

            lax.fori_loop(0, peers, fill, 0)
            pltpu.make_async_copy(relay_send.at[u, j, 0], out_ref.at[origin, :, here, cols], out_sem).start()

            def forward(k, carry):
                send(
                    relay_send.at[u, j, k],
                    out_ref.at[origin, :, here, cols],
                    relay_sem,
                    out_sem,
                    post_id(peer(k)),
                )
                return carry

            lax.fori_loop(1, peers, forward, 0)

    for c in range(chunks):

        @pl.when(is_relay)
        def _():
            for u in range(c * SPANS, (c + 1) * SPANS):
                relay_chunk(u)

        if c == chunks // 2 - 1:
            share_cents()
        if c == chunks // 2:
            rescore()

    wait_bytes(meta_ref, meta_sem)
    wait_bytes(cross_send, cross_sem)
    wait_bytes(near_send.at[:, pl.ds(1, peers - 1)], near_sem)
    wait_bytes(cent_all.at[pl.ds(0, peers)], cent_sem)
    wait_bytes(cent_rep, rep_sem)
    for k in range(n_rep - 1):
        wait_bytes(rows_in.at[k], rows_sem.at[k])
        wait_bytes(cur_in.at[k], cur_sem.at[k])
        wait_bytes(score_own, score_sem.at[k])
        wait_bytes(score_own, score_in_sem.at[k])

    @pl.when(is_relay)
    def _():
        wait_bytes(relay_send.at[:, :, pl.ds(1, peers - 1)], relay_sem)
        wait_bytes(cent_all.at[pl.ds(0, 2 * peers - 2)], cent_fwd_sem)

    wait_bytes(out_ref, out_sem)


def exchange(call_id, cross, near, count, meta, vectors, labels, lengths, residents, n_post, n_rep, hslot):
    neighbour_ids, res_vectors, res_centroids, res_lengths = residents
    s_local, length, dim_share = vectors.shape
    half_rows = length // 2
    n_halves = 2 * s_local
    capacity = cross.shape[0]
    postings = res_vectors.shape[0]
    res_part = postings // n_rep
    peers = n_post // 2
    chunks = half_rows // ROWS
    bf16 = jnp.bfloat16
    in_smem = pl.BlockSpec(memory_space=pltpu.SMEM)
    in_vmem = pl.BlockSpec(memory_space=pltpu.VMEM)
    in_any = pl.BlockSpec(memory_space=pl.ANY)
    dma = pltpu.SemaphoreType.DMA
    return pl.pallas_call(
        exchange_kernel,
        in_specs=[in_smem] * 4 + [in_vmem] * 7,
        out_specs=[in_any, in_vmem, in_vmem, in_vmem],
        out_shape=[
            jax.ShapeDtypeStruct((n_post, hslot, half_rows, dim_share), bf16),
            jax.ShapeDtypeStruct((n_halves, dim_share), jnp.float32),
            jax.ShapeDtypeStruct((n_rep, res_part, length), jnp.float32),
            jax.ShapeDtypeStruct((ROWS, 128), jnp.float32),
        ],
        scratch_shapes=[
            pltpu.VMEM((2,) + meta.shape, jnp.int32),
            pltpu.SMEM((2,) + meta.shape, jnp.int32),
            pltpu.VMEM((n_post, n_halves + ROWS, dim_share), bf16),
            pltpu.VMEM((n_rep - 1, n_post, n_halves + ROWS, dim_share), bf16),
            pltpu.VMEM((n_rep - 1, res_part, length, dim_share), bf16),
            pltpu.VMEM((n_rep - 1, postings, dim_share), bf16),
            pltpu.VMEM((postings, length), jnp.float32),
            pltpu.VMEM((res_part, length), jnp.float32),
            pltpu.VMEM((n_halves, dim_share), jnp.float32),
            pltpu.VMEM((n_halves + 1, ROWS, dim_share), bf16),
            pltpu.VMEM((s_local, length), jnp.int32),
            pltpu.VMEM((2, s_local, length), jnp.float32),
            pltpu.VMEM((chunks * SPANS, capacity, ROWS, dim_share // SPANS), bf16),
            pltpu.VMEM((chunks, peers, hslot, ROWS, dim_share), bf16),
            pltpu.VMEM((chunks * SPANS, 2, peers, hslot, ROWS, dim_share // SPANS), bf16),
            pltpu.VMEM((n_halves + ROWS, dim_share), bf16),
            pltpu.VMEM((2, n_halves + ROWS, dim_share), bf16),
            dma,
            dma,
            dma,
            dma,
            dma,
            dma,
            dma((2,)),
            dma,
            dma,
            dma((n_rep - 1,)),
            dma((chunks * SPANS, 2)),
        ]
        + [dma((n_rep - 1,))] * 6
        + [dma, dma((2,)), dma((2,))]
        + [pltpu.VMEM((2, capacity + 1, ROWS, dim_share // SPANS), bf16)] * (chunks * SPANS),
        compiler_params=pltpu.CompilerParams(
            collective_id=call_id, has_side_effects=True, vmem_limit_bytes=56 * 2**20
        ),
        cost_estimate=pl.CostEstimate(
            flops=4 * n_halves * half_rows * length * dim_share,
            bytes_accessed=2 * vectors.size + 4 * n_post * hslot * half_rows * dim_share,
            transcendentals=0,
        ),
    )(
        cross,
        near,
        count,
        res_lengths,
        meta,
        vectors,
        labels,
        lengths[:, None],
        neighbour_ids,
        res_vectors,
        res_centroids,
    )


def move_kernel(src_ref, dst_ref, room, in_sem, out_sem):
    blocks = src_ref.shape[0]
    for i in range(blocks):
        pltpu.make_async_copy(src_ref.at[i], room.at[i], in_sem.at[i]).start()
    for i in range(blocks):
        pltpu.make_async_copy(src_ref.at[i], room.at[i], in_sem.at[i]).wait()
        pltpu.make_async_copy(room.at[i], dst_ref.at[i], out_sem.at[i]).start()
    for i in range(blocks):
        pltpu.make_async_copy(room.at[i], dst_ref.at[i], out_sem.at[i]).wait()


def move(array):
    return pl.pallas_call(
        move_kernel,
        in_specs=[pl.BlockSpec(memory_space=pl.ANY)],
        out_specs=pl.BlockSpec(memory_space=pl.ANY),
        out_shape=jax.ShapeDtypeStruct(array.shape, array.dtype),
        scratch_shapes=[
            pltpu.VMEM(array.shape, array.dtype),
            pltpu.SemaphoreType.DMA((array.shape[0],)),
            pltpu.SemaphoreType.DMA((array.shape[0],)),
        ],
        compiler_params=pltpu.CompilerParams(vmem_limit_bytes=40 * 2**20),
    )(array)


def pick(mask, values, missing):
    found = jnp.sum(jnp.where(mask, values + 1, 0), axis=-1)
    return jnp.where(found > 0, found - 1, missing).astype(jnp.int32)


def routes(new_owners, n_post, hslot):
    n_halves = new_owners.size
    peers = n_post // 2
    side = lax.axis_index("post") // peers
    owner = new_owners.reshape(-1)
    order = jnp.arange(n_halves)
    is_before = order[None, :] < order[:, None]
    slot = jnp.sum(((owner[:, None] == owner[None, :]) & is_before).astype(jnp.int32), axis=1)
    crossing = owner // peers != side
    rank = jnp.sum((crossing[None, :] & is_before).astype(jnp.int32), axis=1)
    target = owner * hslot + slot
    slots = jnp.arange(peers * hslot)
    cross = pick(jnp.where(crossing, rank, -1)[None, :] == order[:, None], order[None, :], n_halves)
    near = pick(target[None, :] == side * peers * hslot + slots[:, None], order[None, :], n_halves)
    meta = pick(target[None, :] == (1 - side) * peers * hslot + slots[:, None], rank[None, :], n_halves)
    count = jnp.sum(crossing.astype(jnp.int32)).reshape(1)
    return cross, near, meta, count


def body(
    split_vectors,
    split_labels,
    split_lengths,
    new_owners,
    neighbour_ids,
    resident_vectors,
    resident_centroids,
    resident_lengths,
):
    n_post = lax.axis_size("post")
    s_local, length, dim_share = split_vectors.shape
    half_rows = length // 2
    hslot = max(2, 4 * s_local // n_post)
    n_rep = lax.axis_size("rep")
    cross, near, meta, count = routes(new_owners, n_post, hslot)
    n_halves = 2 * s_local

    def with_room(call_id, capacity):
        table = jnp.minimum(meta, capacity)
        table = jnp.broadcast_to(jnp.pad(table, (0, -table.size % 128))[None, :], (8, table.size + -table.size % 128))
        return exchange(
            call_id,
            cross[:capacity],
            near,
            count,
            table,
            split_vectors,
            split_labels,
            split_lengths,
            (neighbour_ids, resident_vectors, resident_centroids, resident_lengths),
            n_post,
            n_rep,
            hslot,
        )

    usual = 45 * n_halves // 64
    stored, centroids, scores, most = with_room(0, usual)
    stored, _ = lax.while_loop(
        lambda state: state[1] > usual,
        lambda state: (with_room(1, n_halves)[0], jnp.float32(0)),
        (stored, most[0, 0]),
    )
    new_postings = move(stored)
    new_centroids = centroids.reshape(s_local, 2, dim_share)
    rescore = scores.reshape(resident_lengths.shape[0], length)
    return (new_postings, new_centroids, rescore)


def solution(mesh):
    return jax.shard_map(
        body,
        mesh=mesh,
        in_specs=(
            P("post", None, "rep"),
            P("post", None),
            P("post"),
            P("post", None),
            P(),
            P("post", None, "rep"),
            P("post", "rep"),
            P("post"),
        ),
        out_specs=(P("post", None, None, "rep"), P("post", None, "rep"), P("post", None)),
        check_vma=False,
    )
```
